32 devices in a mesh: section: 4 (over x, core), expert: 8 (over z, y).
Axes of the slice: x: 2, y: 2, z: 4, core: 2. Of those that a mesh axis runs over, the one named last changes fastest.
Arguments:
- fwd_tokens: bfloat16 [4, 16, 7168], P('section', 'expert'), may hold values from -6 to 6
- fwd_routes: int32 [4, 16, 2], P('section', 'expert'), may hold values from 0 to 3, all different within a row; in each aligned block of 2 rows (0 to 1, 2 to 3, ..., all dimensions but the last counted through in order) at most 2 rows name the same one
- fwd_probs: float32 [4, 16, 2], P('section', 'expert'), may hold values from 0.2 to 1
- bwd_tokens: bfloat16 [4, 16, 7168], P('section', 'expert'), may hold values from -6 to 6
- bwd_routes: int32 [4, 16, 2], P('section', 'expert'), may hold values from 0 to 3, all different within a row; in each aligned block of 2 rows (0 to 1, 2 to 3, ..., all dimensions but the last counted through in order) at most 2 rows name the same one
- bwd_probs: float32 [4, 16, 2], P('section', 'expert'), may hold values from 0.2 to 1
- bwd_grads: bfloat16 [4, 16, 7168], P('section', 'expert'), may hold values from -6 to 6
- w_gate: bfloat16 [7168, 8192], P(None, 'expert'), may hold values from -0.0625 to 0.0625
- w_up: bfloat16 [7168, 8192], P(None, 'expert'), may hold values from -0.0625 to 0.0625
- w_down: bfloat16 [8192, 7168], P('expert'), may hold values from -0.125 to 0.125
Outputs:
- fwd_next: bfloat16 [4, 16, 7168], P('section', 'expert')
- bwd_next: bfloat16 [4, 16, 7168], P('section', 'expert')
The draws below stay inside these ranges and needn't reach their ends.
Inputs may be any that keep to these rules, and one draw needn't show every extreme that they name: `fwd_routes`: each token names 2 different experts; within the 2 tokens of one device, no expert is named by more than 2 tokens, a bound that some block reaches. `bwd_routes`: as for fwd_routes.
All inputs are finite; a program needn't handle non-finite values.
Results may differ from the reference program's by a relative error of at most 0.0058.
Values may be sent and summed in bfloat16 or wider, within the bound.
No kernel may reach another device: no remote copies, remote signals or barrier semaphores. Data moves between devices by JAX's collectives and lax.ppermute only.
A program may use at most 128 MiB of HBM per device.

```python
import math
import jax
import jax.numpy as jnp
import numpy as np
from jax import lax

D = 7168
HIDDEN_SIZE = 2048
GROUPS = 4
TOPK = 2
TOK_DEV = 2
CAP = 2
SHARDS = 2
HID_DEV = 1024
TOKENS = 16
N_SECTION = 4
N_EXPERT = 8


def levels(key, dims, cuts, least, top_value):
    def one(dim, parts):
        heights = jax.random.uniform(jax.random.fold_in(jax.random.fold_in(key, 6), dim), (parts,), jnp.float32, least / len(cuts), top_value / len(cuts))
        return jnp.repeat(jnp.exp(heights), dims[dim] // parts).reshape((-1,) + (1,) * (len(dims) - dim - 1))

    level = one(*cuts[0])
    for cut in cuts[1:]:
        level = level * one(*cut)
    return level


def shared_out(own_key, own, number, rows, amount, top, limit, slope):
    order = jax.random.permutation(own_key, amount)
    packed, usual = portions_of(amount, rows * top, limit, slope, True), portions_of(amount, rows * top, limit, slope, False)
    places = jnp.arange(amount)

    def named(lengths, rotation):
        used = int((lengths > 0).sum())
        fixed = max(1, used // 4)
        shifted = fixed + (places - fixed + rotation * (used - fixed)) % max(1, amount - fixed)
        return jnp.zeros((amount,), jnp.int32).at[order[jnp.where(places < fixed, places, shifted)]].set(jnp.asarray(lengths, jnp.int32))

    lengths = jnp.where(number % 4 == 0, named(packed, number // 4), named(usual, number - number // 4 - 1))
    mixed = jax.random.permutation(jax.random.fold_in(own, 3), amount)
    giver, receiver = mixed[0:amount // 2 * 2:2], mixed[1:amount // 2 * 2:2]
    margin = jnp.minimum(lengths[giver] - 1, limit - lengths[receiver]) // 2
    margin = jnp.where((giver == order[0]) | (receiver == order[0]) | (lengths[receiver] == 0), 0, jnp.maximum(margin, 0))
    shifted = jax.random.randint(jax.random.fold_in(own, 4), (amount // 2,), 0, 1 << 20) % (margin + 1)
    lengths = lengths.at[giver].add(-shifted).at[receiver].add(shifted)
    members = jnp.searchsorted(jnp.cumsum(lengths), jnp.arange(rows * top), side="right").astype(jnp.int32)
    grid = members.reshape(top, rows).T
    grid = grid[jax.random.permutation(jax.random.fold_in(own, 1), rows)]
    rotation = jax.random.randint(jax.random.fold_in(own, 2), (rows, 1), 0, top)
    return jnp.take_along_axis(grid, (jnp.arange(top)[None, :] + rotation) % top, axis=1)


def portions_of(count, total, most, lean, full):
    portions = [(1 << 20) // math.isqrt(grade ** lean) + 1 for grade in range(1, count + 1)]
    largest = most if full else min(most, max(-(-total // count), total * portions[0] // sum(portions)))
    least = 1 if total - largest >= count - 1 else 0
    counts, spare = [largest] + [least] * (count - 1), total - largest - least * (count - 1)
    while spare > 0:
        free = [i for i in range(1, count) if counts[i] < largest] or [i for i in range(1, count) if counts[i] < most]
        whole, budget = sum([portions[i] for i in free]), spare
        for i in free:
            more = min(most - counts[i], max(1, budget * portions[i] // whole), spare)
            counts[i] = counts[i] + more
            spare = spare - more
    return np.array(counts)


def gaussian(own_key, dims, spread, reach, split=(), kind=jnp.bfloat16):
    gain = levels(own_key, dims, split, -0.22, 0.18) if split else 1.0
    result = jax.random.normal(own_key, dims, jnp.float32) * spread * gain
    return jnp.minimum(jnp.maximum(result, -reach), reach).astype(kind)


def setup_inputs(seed: int = 0) -> dict:
    streams_of = jax.random.split(jax.random.key(seed), 11)
    fwd_tokens = gaussian(streams_of[0], (N_SECTION, TOKENS, D), 1.0, 6.0, ((0, 4), (1, 8)))
    fwd_routes_keys = jax.random.split(jax.random.fold_in(streams_of[1], 1), N_SECTION * TOKENS // TOK_DEV)
    fwd_routes_turns = jax.random.permutation(jax.random.fold_in(streams_of[1], 3), N_SECTION * TOKENS // TOK_DEV)
    fwd_routes = jax.vmap(lambda own, number: shared_out(jax.random.fold_in(streams_of[1], 2), own, number, TOK_DEV, GROUPS, TOPK, CAP, 2))(fwd_routes_keys, fwd_routes_turns).reshape((N_SECTION, TOKENS, TOPK))
    fwd_probs = jnp.clip(0.2 + 0.8 * jax.random.uniform(streams_of[2], (N_SECTION, TOKENS, TOPK), jnp.float32) ** levels(streams_of[2], (N_SECTION, TOKENS, TOPK), ((0, 4), (1, 8)), -0.2, 0.2), 0.2, 1.0)
    bwd_tokens = gaussian(streams_of[3], (N_SECTION, TOKENS, D), 1.0, 6.0, ((0, 4), (1, 8)))
    bwd_routes_keys = jax.random.split(jax.random.fold_in(streams_of[4], 1), N_SECTION * TOKENS // TOK_DEV)
    bwd_routes_turns = jax.random.permutation(jax.random.fold_in(streams_of[4], 3), N_SECTION * TOKENS // TOK_DEV)
    bwd_routes = jax.vmap(lambda own, number: shared_out(jax.random.fold_in(streams_of[4], 2), own, number, TOK_DEV, GROUPS, TOPK, CAP, 2))(bwd_routes_keys, bwd_routes_turns).reshape((N_SECTION, TOKENS, TOPK))
    bwd_probs = jnp.clip(0.2 + 0.8 * jax.random.uniform(streams_of[5], (N_SECTION, TOKENS, TOPK), jnp.float32) ** levels(streams_of[5], (N_SECTION, TOKENS, TOPK), ((0, 4), (1, 8)), -0.2, 0.2), 0.2, 1.0)
    bwd_grads = gaussian(streams_of[6], (N_SECTION, TOKENS, D), 1.0, 6.0, ((0, 4), (1, 8)))
    w_gate = gaussian(streams_of[7], (D, GROUPS * HIDDEN_SIZE), D ** -0.5, 0.0625, ((1, 8),))
    w_up = gaussian(streams_of[8], (D, GROUPS * HIDDEN_SIZE), D ** -0.5, 0.0625, ((1, 8),))
    w_down = gaussian(streams_of[9], (GROUPS * HIDDEN_SIZE, D), HIDDEN_SIZE ** -0.5, 0.125, ((0, 8),))
    return {"fwd_tokens": fwd_tokens, "fwd_routes": fwd_routes, "fwd_probs": fwd_probs, "bwd_tokens": bwd_tokens, "bwd_routes": bwd_routes, "bwd_probs": bwd_probs, "bwd_grads": bwd_grads, "w_gate": w_gate, "w_up": w_up, "w_down": w_down}


def slot_layout(routes):
    onehot = (routes[:, :, None] == jnp.arange(GROUPS, dtype=jnp.int32)[None, None, :]).astype(jnp.int32)
    local = onehot.reshape(N_EXPERT, TOK_DEV * TOPK, GROUPS)
    rank = jnp.cumsum(local, axis=1) - local
    own_rank = jnp.sum(rank * local, axis=2).reshape(-1)
    sender = (jnp.arange(TOKENS * TOPK, dtype=jnp.int32) // (TOK_DEV * TOPK)).astype(jnp.int32)
    slot = (sender * CAP + own_rank).astype(jnp.int32)
    return routes.reshape(-1).astype(jnp.int32), slot


def shard_weights(w_gate, w_up, w_down, group):
    wg = w_gate[:, group * HIDDEN_SIZE:(group + 1) * HIDDEN_SIZE].reshape(D, SHARDS, HID_DEV).transpose(1, 0, 2)
    wu = w_up[:, group * HIDDEN_SIZE:(group + 1) * HIDDEN_SIZE].reshape(D, SHARDS, HID_DEV).transpose(1, 0, 2)
    wd = w_down[group * HIDDEN_SIZE:(group + 1) * HIDDEN_SIZE, :].reshape(SHARDS, HID_DEV, D)
    return wg, wu, wd


def expert_forward(rows, weights):
    def step(total, shard):
        wg, wu, wd = shard
        a = jnp.dot(rows, wg, preferred_element_type=jnp.float32)
        u = jnp.dot(rows, wu, preferred_element_type=jnp.float32)
        hidden = (a * jax.nn.sigmoid(a) * u).astype(jnp.bfloat16)
        part = jnp.dot(hidden, wd, preferred_element_type=jnp.float32).astype(jnp.bfloat16)
        return total + part.astype(jnp.float32), None
    total, unused = lax.scan(step, jnp.zeros((rows.shape[0], D), jnp.float32), weights)
    return total


def expert_backward(rows, grads, weights):
    def step(total, shard):
        wg, wu, wd = shard
        a = jnp.dot(rows, wg, preferred_element_type=jnp.float32)
        u = jnp.dot(rows, wu, preferred_element_type=jnp.float32)
        dh = jnp.dot(grads, wd.T, preferred_element_type=jnp.float32)
        sig = jax.nn.sigmoid(a)
        d_a = (dh * u * sig * (1.0 + a * (1.0 - sig))).astype(jnp.bfloat16)
        d_u = (dh * a * sig).astype(jnp.bfloat16)
        part = jnp.dot(d_a, wg.T, preferred_element_type=jnp.float32) + jnp.dot(d_u, wu.T, preferred_element_type=jnp.float32)
        return total + part.astype(jnp.bfloat16).astype(jnp.float32), None
    total, unused = lax.scan(step, jnp.zeros((rows.shape[0], D), jnp.float32), weights)
    return total


def one_section(w_gate, w_up, w_down, pieces):
    fwd_tokens, fwd_routes, fwd_probs, bwd_tokens, bwd_routes, bwd_probs, bwd_grads = pieces
    width = N_EXPERT * CAP
    group_f, slot_f = slot_layout(fwd_routes)
    group_b, slot_b = slot_layout(bwd_routes)
    rows_f = jnp.broadcast_to(fwd_tokens[:, None, :], (TOKENS, TOPK, D)).reshape(-1, D)
    rows_b = jnp.broadcast_to(bwd_tokens[:, None, :], (TOKENS, TOPK, D)).reshape(-1, D)
    rows_g = jnp.broadcast_to(bwd_grads[:, None, :], (TOKENS, TOPK, D)).reshape(-1, D)
    empty = jnp.zeros((GROUPS, width, D), jnp.bfloat16)
    buf_f = empty.at[group_f, slot_f].set(rows_f)
    buf_b = empty.at[group_b, slot_b].set(rows_b)
    buf_g = empty.at[group_b, slot_b].set(rows_g)
    outs_f = []
    outs_b = []
    for group in range(GROUPS):
        weights = shard_weights(w_gate, w_up, w_down, group)
        outs_f.append(expert_forward(buf_f[group], weights))
        outs_b.append(expert_backward(buf_b[group], buf_g[group], weights))
    outs_f = jnp.stack(outs_f)
    outs_b = jnp.stack(outs_b)
    got_f = outs_f[group_f, slot_f].reshape(TOKENS, TOPK, D)
    got_b = outs_b[group_b, slot_b].reshape(TOKENS, TOPK, D)
    layer_out = jnp.sum(got_f * fwd_probs[:, :, None], axis=1).astype(jnp.bfloat16)
    input_grad = jnp.sum(got_b * bwd_probs[:, :, None], axis=1).astype(jnp.bfloat16)
    return layer_out, input_grad


def reference(fwd_tokens, fwd_routes, fwd_probs, bwd_tokens, bwd_routes, bwd_probs, bwd_grads, w_gate, w_up, w_down):
    layer_out, input_grad = lax.map(
        lambda pieces: one_section(w_gate, w_up, w_down, pieces),
        (fwd_tokens, fwd_routes, fwd_probs, bwd_tokens, bwd_routes, bwd_probs, bwd_grads))
    zeros = jnp.zeros((1, TOKENS, D), jnp.bfloat16)
    fwd_next = jnp.concatenate([zeros, layer_out[:-1]], axis=0)
    bwd_next = jnp.concatenate([input_grad[1:], zeros], axis=0)
    return fwd_next, bwd_next
```

```python
import functools

import jax
import jax.numpy as jnp
from jax import lax
from jax.experimental import pallas as pl
from jax.experimental.pallas import tpu as pltpu
from jax.sharding import PartitionSpec as P

GROUPS = 4
TILE = 256
F32 = jnp.float32
BF16 = jnp.bfloat16
NT = (((1,), (1,)), ((), ()))


def swap_cores(block):
    sections = range(lax.axis_size("section"))
    return lax.ppermute(block, "section", [(i, i ^ 1) for i in sections])


def shifted(block, distance):
    sections = range(lax.axis_size("section"))
    route = [(i - distance, i) for i in sections if i - distance in sections]
    return lax.ppermute(block, "section", route)


def expert_weights(routes, probs):
    named = routes[:, :, None] == jnp.arange(GROUPS, dtype=jnp.int32)
    return jnp.sum(jnp.where(named, probs[:, :, None], 0.0), axis=1)


def halves(rows, core):
    half = rows.shape[1] // 2
    first, second = rows[:, :half], rows[:, half:]
    return jnp.where(core == 0, first, second), jnp.where(core == 0, second, first)


def by_section(own, other, core):
    return jnp.where(core == 0, jnp.stack([own, other]), jnp.stack([other, own]))


def to_all(block):
    spread = jnp.broadcast_to(block[None], (lax.axis_size("expert"),) + block.shape)
    return lax.all_to_all(spread, "expert", split_axis=0, concat_axis=0, tiled=True)


def interleave(count, inverse=False):
    blocks = count // 8
    out = lax.broadcasted_iota(jnp.int32, (count, count), 1 if inverse else 0)
    src = lax.broadcasted_iota(jnp.int32, (count, count), 0 if inverse else 1)
    want = lax.rem(lax.div(out, 4), 2) * (blocks * 4) + lax.div(out, 8) * 4 + lax.rem(out, 4)
    return jnp.where(want == src, 1.0, 0.0).astype(BF16)


def dot(a, b):
    return jnp.dot(a, b, preferred_element_type=F32)


def dot_nt(a, b):
    return lax.dot_general(a, b, NT, preferred_element_type=F32)


def fwd_up_kernel(core, x, wg0, wg1, wu0, wu1, out):
    n = x.shape[0] // 2
    hid = wg0.shape[1]
    rows = dot(interleave(2 * n, True), x[...]).astype(BF16)
    a = dot(rows[:n], wg0[...]) + dot(rows[n:], wg1[...])
    u = dot(rows[:n], wu0[...]) + dot(rows[n:], wu1[...])

    @pl.when(pl.program_id(0) == 0)
    def _():
        out[...] = jnp.zeros_like(out)

    out[:, :hid] += a
    out[:, hid:] += u


def bwd_up_kernel(core, x0, x1, wg0, wg1, wu0, wu1, wd0, wd1, out):
    n = x0.shape[0] // 2
    hid = wg0.shape[1]
    sel = interleave(2 * n, True)
    rows0 = dot(sel, x0[...]).astype(BF16)
    rows1 = dot(sel, x1[...]).astype(BF16)
    a = dot(rows0[:n], wg0[...]) + dot(rows1[:n], wg1[...])
    u = dot(rows0[:n], wu0[...]) + dot(rows1[:n], wu1[...])
    dh = dot_nt(rows0[n:], wd0[...]) + dot_nt(rows1[n:], wd1[...])

    @pl.when(pl.program_id(0) == 0)
    def _():
        out[...] = jnp.zeros_like(out)

    out[:, :hid] += a
    out[:, hid : 2 * hid] += u
    out[:, 2 * hid :] += dh


def fwd_down_kernel(core, part, other, wd0, wd1, out, h):
    hid = h.shape[1]

    @pl.when(pl.program_id(0) == 0)
    def _():
        both = part[...] + other[...]
        a, u = both[:, :hid], both[:, hid:]
        h[...] = (a * jax.nn.sigmoid(a) * u).astype(BF16)

    y0 = dot(h[...], wd0[...]).astype(BF16)
    y1 = dot(h[...], wd1[...]).astype(BF16)
    cat = jnp.concatenate([y0, y1], axis=0)
    out[...] = dot(interleave(cat.shape[0]), cat).astype(BF16)


def bwd_down_kernel(core, part, other, wg0, wg1, wu0, wu1, out, da, du):
    hid = da.shape[1]

    @pl.when(pl.program_id(0) == 0)
    def _():
        both = part[...] + other[...]
        a, u, dh = both[:, :hid], both[:, hid : 2 * hid], both[:, 2 * hid :]
        s = jax.nn.sigmoid(a)
        da[...] = (dh * u * s * (1.0 + a * (1.0 - s))).astype(BF16)
        du[...] = (dh * a * s).astype(BF16)

    y0 = (dot_nt(da[...], wg0[...]) + dot_nt(du[...], wu0[...])).astype(BF16)
    y1 = (dot_nt(da[...], wg1[...]) + dot_nt(du[...], wu1[...])).astype(BF16)
    cat = jnp.concatenate([y0, y1], axis=0)
    out[...] = dot(interleave(cat.shape[0]), cat).astype(BF16)


def run(kernel, core, steps, operands, specs, out_spec, out_shape, scratch, flops):
    nbytes = sum(b * 2 * steps for b in flops)
    return pl.pallas_call(
        kernel,
        grid_spec=pltpu.PrefetchScalarGridSpec(
            num_scalar_prefetch=1,
            grid=(steps,),
            in_specs=specs,
            out_specs=out_spec,
            scratch_shapes=scratch,
        ),
        out_shape=out_shape,
        compiler_params=pltpu.CompilerParams(vmem_limit_bytes=48 * 2**20),
        cost_estimate=pl.CostEstimate(
            flops=nbytes * 64, bytes_accessed=nbytes, transcendentals=0
        ),
    )(core, *operands)


def local(
    fwd_tokens,
    fwd_routes,
    fwd_probs,
    bwd_tokens,
    bwd_routes,
    bwd_probs,
    bwd_grads,
    w_gate,
    w_up,
    w_down,
):
    ranks = lax.axis_size("expert")
    shards = ranks // GROUPS
    width = fwd_tokens.shape[2]
    hid = w_gate.shape[1]
    quarter = width // 4
    steps = quarter // TILE
    core = lax.axis_index("section") % 2
    which = core.astype(jnp.int32).reshape(1)
    rows = 4 * ranks

    keep, send = halves(jnp.concatenate([bwd_tokens[0], bwd_grads[0]]), core)
    pair = by_section(keep, swap_cores(send), core)
    block_b = jnp.concatenate([pair[:, :2].reshape(4, -1), pair[:, 2:].reshape(4, -1)])
    got_b = to_all(block_b).reshape(2 * rows, width // 2)

    moved = shifted(fwd_tokens[0], 1)
    keep, send = halves(moved, core)
    block_f = by_section(keep, swap_cores(send), core).reshape(4, 2, quarter)
    block_f = block_f.transpose(1, 0, 2).reshape(8, quarter)
    got_f = to_all(block_f).reshape(2 * rows, quarter)

    weights = jnp.stack(
        [
            shifted(expert_weights(fwd_routes[0], fwd_probs[0]), 1),
            expert_weights(bwd_routes[0], bwd_probs[0]),
        ]
    )
    weights = by_section(weights, swap_cores(weights), core)
    weights = weights.transpose(1, 3, 0, 2).reshape(2, GROUPS, 1, 1, 4)
    weights = jnp.broadcast_to(weights, (2, GROUPS, shards, 2, 4)).reshape(2, ranks, 8, 1)

    def tall(q):
        return pl.BlockSpec((TILE, hid), lambda k, c: ((2 * c[0] + q) * steps + k, 0))

    def wide(q):
        return pl.BlockSpec((hid, TILE), lambda k, c: (0, (2 * c[0] + q) * steps + k))

    def cols(q):
        return pl.BlockSpec((2 * rows, TILE), lambda k, c: (0, q * steps + k))

    def whole(n):
        return pl.BlockSpec((rows, n * hid), lambda k, c: (0, 0))

    part_b = run(
        bwd_up_kernel,
        which,
        steps,
        (got_b, got_b, w_gate, w_gate, w_up, w_up, w_down, w_down),
        [cols(0), cols(1), tall(0), tall(1), tall(0), tall(1), wide(0), wide(1)],
        whole(3),
        jax.ShapeDtypeStruct((rows, 3 * hid), F32),
        [],
        [6 * TILE * hid],
    )
    out_b = run(
        bwd_down_kernel,
        which,
        steps,
        (part_b, swap_cores(part_b), w_gate, w_gate, w_up, w_up),
        [whole(3), whole(3), tall(0), tall(1), tall(0), tall(1)],
        cols(0),
        jax.ShapeDtypeStruct((2 * rows, quarter), BF16),
        [pltpu.VMEM((rows, hid), BF16)] * 2,
        [4 * TILE * hid],
    )
    back_b = lax.all_to_all(
        out_b.reshape(ranks, 8, quarter), "expert", split_axis=0, concat_axis=0, tiled=True
    )

    part_f = run(
        fwd_up_kernel,
        which,
        steps,
        (got_f, w_gate, w_gate, w_up, w_up),
        [cols(0), tall(0), tall(1), tall(0), tall(1)],
        whole(2),
        jax.ShapeDtypeStruct((rows, 2 * hid), F32),
        [],
        [4 * TILE * hid],
    )
    out_f = run(
        fwd_down_kernel,
        which,
        steps,
        (part_f, swap_cores(part_f), w_down, w_down),
        [whole(2), whole(2), wide(0), wide(1)],
        cols(0),
        jax.ShapeDtypeStruct((2 * rows, quarter), BF16),
        [pltpu.VMEM((rows, hid), BF16)],
        [2 * TILE * hid],
    )
    back_f = lax.all_to_all(
        out_f.reshape(ranks, 8, quarter), "expert", split_axis=0, concat_axis=0, tiled=True
    )

    def finished(back, weight):
        total = jnp.sum(back.astype(F32) * weight, axis=0).astype(BF16)
        both = total.reshape(2, 2, 2, quarter).transpose(1, 2, 0, 3).reshape(2, 2, width // 2)
        own = jnp.where(core == 0, both[0], both[1])
        other = swap_cores(jnp.where(core == 0, both[1], both[0]))
        return jnp.where(
            core == 0,
            jnp.concatenate([own, other], axis=1),
            jnp.concatenate([other, own], axis=1),
        )

    bwd_next = shifted(finished(back_b, weights[1]), -1)
    fwd_next = finished(back_f, weights[0])
    return (fwd_next[None], bwd_next[None])


def solution(mesh):
    return jax.shard_map(
        local,
        mesh=mesh,
        in_specs=(
            P("section", "expert", None),
            P("section", "expert", None),
            P("section", "expert", None),
            P("section", "expert", None),
            P("section", "expert", None),
            P("section", "expert", None),
            P("section", "expert", None),
            P(None, "expert"),
            P(None, "expert"),
            P("expert", None),
        ),
        out_specs=(P("section", "expert", None), P("section", "expert", None)),
        check_vma=False,
    )
```

```python
import functools

import jax
import jax.numpy as jnp
from jax import lax
from jax.experimental import pallas as pl
from jax.experimental.pallas import tpu as pltpu
from jax.sharding import PartitionSpec as P

GROUPS = 4
LANES = 128
PARTS = 4
F32 = jnp.float32
BF16 = jnp.bfloat16
NT = (((1,), (1,)), ((), ()))


def swap_cores(block):
    sections = range(lax.axis_size("section"))
    return lax.ppermute(block, "section", [(i, i ^ 1) for i in sections])


def swap_chips(block):
    odd = range(1, lax.axis_size("section") - 1, 2)
    return lax.ppermute(block, "section", [(i, i + 1) for i in odd] + [(i + 1, i) for i in odd])


def expert_weights(routes, probs):
    named = routes[:, :, None] == jnp.arange(GROUPS, dtype=jnp.int32)
    return jnp.sum(jnp.where(named, probs[:, :, None], 0.0), axis=1)


def as_lanes(weights, rows):
    high = lax.reduce_precision(weights, 8, 7)
    middle = lax.reduce_precision(weights - high, 8, 7)
    low = weights - high - middle
    terms = jnp.concatenate([high, middle, low], axis=1).astype(BF16)
    return jnp.pad(terms, ((0, rows - terms.shape[0]), (0, LANES - terms.shape[1])))


def from_lanes(block):
    terms = block[:2, : 3 * GROUPS].astype(F32)
    return terms[:, :GROUPS] + terms[:, GROUPS : 2 * GROUPS] + terms[:, 2 * GROUPS :]


def split_width(message, core):
    width = message.shape[1] - LANES
    half = width // 2
    first, second, lanes = message[:, :half], message[:, half:width], message[:, width:]
    keep = jnp.where(core == 0, first, second)
    send = jnp.where(core == 0, second, first)
    got = swap_cores(jnp.concatenate([send, lanes], axis=1))
    fwd = jnp.where(core == 0, keep, got[:, :half])[:2]
    bwd = jnp.where(core == 0, got[:, :half], keep)
    mine, theirs = from_lanes(lanes), from_lanes(got[:, half:])
    return (
        jnp.concatenate([fwd, bwd]),
        jnp.where(core == 0, mine, theirs),
        jnp.where(core == 0, theirs, mine),
    )


def to_all(block):
    rows, width = block.shape
    block = block.reshape(rows, PARTS, width // PARTS).transpose(1, 0, 2)
    block = block.reshape(1, rows * PARTS, width // PARTS)
    ranks = lax.axis_size("expert")
    spread = jnp.broadcast_to(block, (ranks,) + block.shape[1:])
    got = lax.all_to_all(spread, "expert", split_axis=0, concat_axis=0, tiled=True)
    return got.reshape(ranks * rows * PARTS, width // PARTS)


def dot(a, b):
    return jnp.dot(a, b, preferred_element_type=F32)


def dot_nt(a, b):
    return lax.dot_general(a, b, NT, preferred_element_type=F32)


def gathered_order(ranks):
    count = ranks * PARTS * 6
    out = lax.broadcasted_iota(jnp.int32, (count, count), 0)
    src = lax.broadcasted_iota(jnp.int32, (count, count), 1)
    part, rest = lax.div(out, 6 * ranks), lax.rem(out, 6 * ranks)
    kind, rest = lax.div(rest, 2 * ranks), lax.rem(rest, 2 * ranks)
    want = lax.div(rest, 2) * (6 * PARTS) + part * 6 + kind * 2 + lax.rem(rest, 2)
    return jnp.where(want == src, 1.0, 0.0).astype(BF16)


def returned_order(ranks):
    count = ranks * 8
    out = lax.broadcasted_iota(jnp.int32, (count, count), 0)
    src = lax.broadcasted_iota(jnp.int32, (count, count), 1)
    want = lax.div(lax.rem(out, 8), 2) * (2 * ranks) + lax.div(out, 8) * 2 + lax.rem(out, 2)
    return jnp.where(want == src, 1.0, 0.0).astype(BF16)


def fetch_kernel(core, wg, wu, wd, g, u, d, sems):
    half = g.shape[0]
    start = pl.multiple_of(core[0] * half, half)
    copies = [
        pltpu.make_async_copy(wg.at[pl.ds(start, half)], g, sems.at[0]),
        pltpu.make_async_copy(wu.at[pl.ds(start, half)], u, sems.at[1]),
        pltpu.make_async_copy(wd.at[:, pl.ds(start, half)], d, sems.at[2]),
    ]
    for copy in copies:
        copy.start()
    for copy in copies:
        copy.wait()


def fetch(core, w_gate, w_up, w_down):
    width, hid = w_gate.shape
    half = width // 2
    return pl.pallas_call(
        fetch_kernel,
        in_specs=[pl.BlockSpec(memory_space=pltpu.SMEM)]
        + [pl.BlockSpec(memory_space=pl.ANY)] * 3,
        out_specs=[pl.BlockSpec(memory_space=pltpu.VMEM)] * 3,
        out_shape=[
            pltpu.VMEM((half, hid), BF16),
            pltpu.VMEM((half, hid), BF16),
            pltpu.VMEM((hid, half), BF16),
        ],
        scratch_shapes=[pltpu.SemaphoreType.DMA((3,))],
        compiler_params=pltpu.CompilerParams(vmem_limit_bytes=32 * 2**20),
        cost_estimate=pl.CostEstimate(
            flops=0, bytes_accessed=6 * half * hid * 2, transcendentals=0
        ),
    )(core, w_gate, w_up, w_down)


def up_kernel(ranks, near, far, g, u, d, out):
    hid = g.shape[1]
    n = 2 * ranks
    piece = near.shape[1]
    order = gathered_order(ranks)
    near_rows = dot(order, near[...]).astype(BF16)
    far_rows = dot(order, far[...]).astype(BF16)
    a, b, dh = 0.0, 0.0, 0.0
    for part in range(PARTS):
        at = part * 3 * n
        cols = slice(part * piece, (part + 1) * piece)
        rows = jnp.concatenate(
            [
                near_rows[at : at + n],
                far_rows[at : at + n],
                near_rows[at + n : at + 2 * n],
                far_rows[at + n : at + 2 * n],
            ]
        )
        grads = jnp.concatenate(
            [near_rows[at + 2 * n : at + 3 * n], far_rows[at + 2 * n : at + 3 * n]]
        )
        a += dot(rows, g[cols, :])
        b += dot(rows, u[cols, :])
        dh += dot_nt(grads, d[:, cols])
    out[:, :hid] = a[: 2 * n]
    out[:, hid : 2 * hid] = b[: 2 * n]
    out[:, 2 * hid : 3 * hid] = a[2 * n :]
    out[:, 3 * hid : 4 * hid] = b[2 * n :]
    out[:, 4 * hid :] = dh


def down_kernel(ranks, mine, theirs, g, u, d, out):
    hid = g.shape[1]
    a = mine[:, :hid] + theirs[:, :hid]
    b = mine[:, hid : 2 * hid] + theirs[:, hid : 2 * hid]
    h = (a * jax.nn.sigmoid(a) * b).astype(BF16)
    a = mine[:, 2 * hid : 3 * hid] + theirs[:, 2 * hid : 3 * hid]
    b = mine[:, 3 * hid : 4 * hid] + theirs[:, 3 * hid : 4 * hid]
    dh = mine[:, 4 * hid :] + theirs[:, 4 * hid :]
    s = jax.nn.sigmoid(a)
    da = (dh * b * s * (1.0 + a * (1.0 - s))).astype(BF16)
    du = (dh * a * s).astype(BF16)
    order = returned_order(ranks)
    piece = out.shape[1] // PARTS
    for part in range(PARTS):
        cols = slice(part * piece, (part + 1) * piece)
        y = dot(h, d[:, cols])
        dx = dot_nt(da, g[cols, :]) + dot_nt(du, u[cols, :])
        rows = jnp.concatenate([y.astype(BF16), dx.astype(BF16)])
        out[:, cols] = dot(order, rows).astype(BF16)


def on_core(kernel, operands, shape, dtype, passes, weight):
    return pl.pallas_call(
        kernel,
        in_specs=[pl.BlockSpec(memory_space=pltpu.VMEM)] * len(operands),
        out_specs=pl.BlockSpec(memory_space=pltpu.VMEM),
        out_shape=jax.ShapeDtypeStruct(shape, dtype),
        compiler_params=pltpu.CompilerParams(vmem_limit_bytes=12 * 2**20),
        cost_estimate=pl.CostEstimate(
            flops=passes * 2 * weight.size * 256,
            bytes_accessed=passes * weight.size * 2,
            transcendentals=0,
        ),
    )(*operands)


def local(
    fwd_tokens,
    fwd_routes,
    fwd_probs,
    bwd_tokens,
    bwd_routes,
    bwd_probs,
    bwd_grads,
    w_gate,
    w_up,
    w_down,
):
    ranks = lax.axis_size("expert")
    shards = ranks // GROUPS
    width = fwd_tokens.shape[2]
    hid = w_gate.shape[1]
    core = lax.axis_index("section") % 2

    fwd = jnp.concatenate(
        [
            jnp.pad(fwd_tokens[0], ((0, 2), (0, 0))),
            as_lanes(expert_weights(fwd_routes[0], fwd_probs[0]), 4),
        ],
        axis=1,
    )
    bwd = jnp.concatenate(
        [
            jnp.concatenate([bwd_tokens[0], bwd_grads[0]]),
            as_lanes(expert_weights(bwd_routes[0], bwd_probs[0]), 4),
        ],
        axis=1,
    )
    near, near_fw, near_bw = split_width(jnp.where(core == 0, fwd, bwd), core)
    far, far_fw, far_bw = split_width(swap_chips(jnp.where(core == 0, bwd, fwd)), core)
    got_near = to_all(near)
    got_far = to_all(far)

    which, _ = lax.optimization_barrier((core.astype(jnp.int32).reshape(1), near))
    g, u, d = fetch(which, w_gate, w_up, w_down)
    part = on_core(
        functools.partial(up_kernel, ranks),
        (got_near, got_far, g, u, d),
        (4 * ranks, 5 * hid),
        F32,
        3,
        g,
    )
    out = on_core(
        functools.partial(down_kernel, ranks),
        (part, swap_cores(part), g, u, d),
        (8 * ranks, width // 2),
        BF16,
        3,
        g,
    )
    back = lax.all_to_all(
        out.reshape(ranks, 8, width // 2), "expert", split_axis=0, concat_axis=0, tiled=True
    )

    weights = jnp.concatenate([near_fw, far_fw, near_bw, far_bw]).T[:, None]
    weights = jnp.broadcast_to(weights, (GROUPS, shards, 8)).reshape(ranks, 8, 1)
    total = jnp.sum(back.astype(F32) * weights, axis=0).astype(BF16)
    first = jnp.concatenate([total[2:4], total[4:6]])
    second = jnp.concatenate([total[:2], total[6:]])
    own = jnp.where(core == 0, first, second)
    other = swap_cores(jnp.where(core == 0, second, first))
    whole = jnp.where(
        core == 0,
        jnp.concatenate([own, other], axis=1),
        jnp.concatenate([other, own], axis=1),
    )
    return (whole[None, :2], whole[None, 2:])


def solution(mesh):
    return jax.shard_map(
        local,
        mesh=mesh,
        in_specs=(
            P("section", "expert", None),
            P("section", "expert", None),
            P("section", "expert", None),
            P("section", "expert", None),
            P("section", "expert", None),
            P("section", "expert", None),
            P("section", "expert", None),
            P(None, "expert"),
            P(None, "expert"),
            P("expert", None),
        ),
        out_specs=(P("section", "expert", None), P("section", "expert", None)),
        check_vma=False,
    )
```

```python
import functools

import jax
import jax.numpy as jnp
from jax import lax
from jax.experimental import pallas as pl
from jax.experimental.pallas import tpu as pltpu
from jax.sharding import PartitionSpec as P

GROUPS = 4
PARTS = 4
BATCH = 8
F32 = jnp.float32
BF16 = jnp.bfloat16


def swap_cores(block):
    sections = range(lax.axis_size("section"))
    return lax.ppermute(block, "section", [(i, i ^ 1) for i in sections])


def expert_weights(routes, probs):
    named = routes[:, :, None] == jnp.arange(GROUPS, dtype=jnp.int32)
    return jnp.sum(jnp.where(named, probs[:, :, None], 0.0), axis=1)


def by_section(mine, theirs, core):
    return jnp.where(core == 0, mine, theirs), jnp.where(core == 0, theirs, mine)


def swap_ranks(block, bit):
    ranks = range(lax.axis_size("expert"))
    return lax.ppermute(block, "expert", [(i, i ^ bit) for i in ranks])


def to_next_chips(fwd, bwd, bit):
    sections, ranks = lax.axis_size("section"), lax.axis_size("expert")

    def move(block, pairs):
        route = [(a * ranks + e, b * ranks + (e ^ bit)) for a, b in pairs for e in range(ranks)]
        return lax.ppermute(block, ("section", "expert"), route)

    up = [(i, i + 2) for i in range(sections - 2)]
    down = [(b, a) for a, b in up]
    if sections != 4:
        return jnp.concatenate([move(fwd, up), move(bwd, down)])
    first = lax.axis_index("section") < 2
    rows = bwd.shape[0]
    padded = jnp.pad(fwd, ((0, rows - fwd.shape[0]), (0, 0)))
    got = move(jnp.where(first, padded, bwd), up + down)
    none = jnp.zeros_like(got)
    return jnp.concatenate(
        [jnp.where(first, none, got)[: fwd.shape[0]], jnp.where(first, got, none)]
    )


def folded(block):
    rows, width = block.shape
    block = block.reshape(rows, PARTS, width // PARTS).transpose(1, 0, 2)
    return block.reshape(rows * PARTS, width // PARTS)


def dot(a, b):
    return jnp.dot(a, b, preferred_element_type=F32)


def one_hot(want, src):
    return jnp.where(want == src, 1.0, 0.0).astype(BF16)


def gathered_order():
    count = 2 * BATCH * PARTS * 6
    out = lax.broadcasted_iota(jnp.int32, (count, count), 0)
    src = lax.broadcasted_iota(jnp.int32, (count, count), 1)
    part, rest = lax.div(out, 12 * BATCH), lax.rem(out, 12 * BATCH)
    kind, rest = lax.div(rest, 4 * BATCH), lax.rem(rest, 4 * BATCH)
    row = jnp.where(kind == 0, part * 2, part * 4 + kind * 2 + 2 * PARTS - 2)
    want = lax.div(rest, 2) * (6 * PARTS) + row + lax.rem(rest, 2)
    return one_hot(want, src)


def returned_order(ranks, me):
    count = ranks * 8
    out = lax.broadcasted_iota(jnp.int32, (count, count), 0)
    src = lax.broadcasted_iota(jnp.int32, (count, count), 1)
    apart = lax.bitwise_xor(lax.div(out, 8), jnp.full((count, count), me, jnp.int32))
    place = jnp.zeros_like(out)
    for _ in range(ranks.bit_length() - 1):
        place = place * 2 + lax.rem(apart, 2)
        apart = lax.div(apart, 2)
    kind = lax.div(lax.rem(out, 8), 4)
    want = kind * (4 * ranks) + place * 4 + lax.rem(out, 4)
    return one_hot(want, src)


def fetch_kernel(steps, axis, place, weight, earlier, held, turned, zero, sems):
    size = held.shape[axis] // steps
    base = place[0] * held.shape[axis]

    def at(start):
        rows = pl.ds(pl.multiple_of(start, 128), size)
        return rows if axis == 0 else (slice(None), rows)

    copies = [
        pltpu.make_async_copy(
            weight.at[at(base + i * size)], held.at[at(i * size)], sems.at[i]
        )
        for i in range(steps)
    ]
    for copy in copies:
        copy.start()
    for i, copy in enumerate(copies):
        copy.wait()
        here = slice(i * size, (i + 1) * size)
        if axis == 0:
            turned[:, here] = held[here, :].T
        else:
            turned[here, :] = held[:, here].T
    zero[...] = jnp.zeros_like(zero)


def fetch(place, weight, axis, earlier, like):
    steps = 4
    shape = list(weight.shape)
    shape[axis] //= 2
    return pl.pallas_call(
        functools.partial(fetch_kernel, steps, axis),
        in_specs=[
            pl.BlockSpec(memory_space=pltpu.SMEM),
            pl.BlockSpec(memory_space=pltpu.HBM),
            pl.BlockSpec(memory_space=pl.ANY),
        ],
        out_specs=[pl.BlockSpec(memory_space=pltpu.VMEM)] * 3,
        out_shape=[
            pltpu.VMEM(tuple(shape), BF16),
            pltpu.VMEM(tuple(shape[::-1]), BF16),
            jax.ShapeDtypeStruct(like, BF16),
        ],
        scratch_shapes=[pltpu.SemaphoreType.DMA((steps,))],
        compiler_params=pltpu.CompilerParams(vmem_limit_bytes=2**20),
        cost_estimate=pl.CostEstimate(
            flops=0, bytes_accessed=weight.size * 4, transcendentals=0
        ),
    )(place, pltpu.with_memory_space_constraint(weight, pltpu.HBM), earlier)


def up_kernel(ranks, first, second, third, fourth, g, u, d_t, out):
    hid = g.shape[1]
    n = 4 * BATCH
    piece = first.shape[1]
    blocks = jnp.concatenate([first[...], second[...], third[...], fourth[...]])
    order = gathered_order()
    count = order.shape[0]
    batches = ranks // BATCH
    sorted_rows = [
        dot(order, blocks[i * count : (i + 1) * count]).astype(BF16) for i in range(batches)
    ]
    a, b, dh = 0.0, 0.0, 0.0
    for part in range(PARTS):
        at = part * 3 * n
        cols = slice(part * piece, (part + 1) * piece)
        kinds = [
            jnp.concatenate([rows[at + k * n : at + (k + 1) * n] for rows in sorted_rows])
            for k in range(3)
        ]
        rows = jnp.concatenate(kinds[:2])
        a += dot(rows, g[cols, :])
        b += dot(rows, u[cols, :])
        dh += dot(kinds[2], d_t[cols, :])
    n = n * batches
    out[:, :hid] = a[:n]
    out[:, hid : 2 * hid] = b[:n]
    out[:, 2 * hid : 3 * hid] = a[n:]
    out[:, 3 * hid : 4 * hid] = b[n:]
    out[:, 4 * hid :] = dh


def down_kernel(ranks, place, mine, theirs, g_t, u_t, d, out):
    hid = d.shape[0]
    a = mine[:, :hid] + theirs[:, :hid]
    b = mine[:, hid : 2 * hid] + theirs[:, hid : 2 * hid]
    h = (a * jax.nn.sigmoid(a) * b).astype(BF16)
    a = mine[:, 2 * hid : 3 * hid] + theirs[:, 2 * hid : 3 * hid]
    b = mine[:, 3 * hid : 4 * hid] + theirs[:, 3 * hid : 4 * hid]
    dh = mine[:, 4 * hid :] + theirs[:, 4 * hid :]
    s = jax.nn.sigmoid(a)
    da = (dh * b * s * (1.0 + a * (1.0 - s))).astype(BF16)
    du = (dh * a * s).astype(BF16)
    order = returned_order(ranks, place[1])
    piece = out.shape[1] // PARTS
    for part in range(PARTS):
        cols = slice(part * piece, (part + 1) * piece)
        y = dot(h, d[:, cols])
        dx = dot(da, g_t[:, cols]) + dot(du, u_t[:, cols])
        rows = jnp.concatenate([y.astype(BF16), dx.astype(BF16)])
        out[:, cols] = dot(order, rows).astype(BF16)


def on_core(kernel, ranks, scalars, operands, results, weight):
    return pl.pallas_call(
        kernel,
        in_specs=[pl.BlockSpec(memory_space=pltpu.SMEM)] * len(scalars)
        + [pl.BlockSpec(memory_space=pltpu.VMEM)] * len(operands),
        out_specs=[pl.BlockSpec(memory_space=pltpu.VMEM)] * len(results),
        out_shape=[jax.ShapeDtypeStruct(*result) for result in results],
        compiler_params=pltpu.CompilerParams(vmem_limit_bytes=ranks * 2**18),
        cost_estimate=pl.CostEstimate(
            flops=6 * weight.size * 256, bytes_accessed=6 * weight.size, transcendentals=0
        ),
    )(*scalars, *[pltpu.with_memory_space_constraint(x, pltpu.VMEM) for x in operands])


def after(value, other):
    return lax.optimization_barrier((value, other))[0]


def local(
    fwd_tokens,
    fwd_routes,
    fwd_probs,
    bwd_tokens,
    bwd_routes,
    bwd_probs,
    bwd_grads,
    w_gate,
    w_up,
    w_down,
):
    ranks = lax.axis_size("expert")
    shards = ranks // GROUPS
    width = fwd_tokens.shape[2]
    half = width // 2
    hid = w_gate.shape[1]
    core = lax.axis_index("section") % 2
    place = jnp.stack([core, lax.axis_index("expert")]).astype(jnp.int32)

    rows = jnp.concatenate([fwd_tokens[0], bwd_tokens[0], bwd_grads[0]])
    first, second = rows[:, :half], rows[:, half:]
    keep, send = by_section(first, second, core)
    even, odd = by_section(keep, swap_cores(send), core)

    near = jnp.concatenate([folded(even[:2]), folded(odd[2:])])
    far_fwd, far_bwd = folded(odd[:2]), folded(even[2:])
    top = ranks // 2
    far = to_next_chips(far_fwd, far_bwd, 0)
    far_top = to_next_chips(far_fwd, far_bwd, top)
    blocks = jnp.concatenate([near, far, swap_ranks(near, top), far_top])
    g, g_t, zero = fetch(place, w_gate, 0, near, blocks.shape)
    blocks = blocks + zero
    bit = top // 2
    while bit > 2:
        blocks = jnp.concatenate([blocks, swap_ranks(blocks, bit)])
        bit //= 2
    second = swap_ranks(blocks, 2)
    third = swap_ranks(blocks, 1)
    u, u_t, zero = fetch(place, w_up, 0, blocks, second.shape)
    second = second + zero
    fourth = swap_ranks(second, 1)
    d, d_t, _ = fetch(place, w_down, 1, second, (16, 128))

    (mine,) = on_core(
        functools.partial(up_kernel, ranks),
        ranks,
        (),
        (blocks, second, third, fourth, g, u, d_t),
        [((4 * ranks, 5 * hid), F32)],
        g,
    )
    (out,) = on_core(
        functools.partial(down_kernel, ranks),
        ranks,
        (place,),
        (mine, swap_cores(mine), g_t, u_t, d),
        [((8 * ranks, half), BF16)],
        g,
    )
    back = lax.all_to_all(
        out.reshape(ranks, 8, half), "expert", split_axis=0, concat_axis=0, tiled=True
    )

    weights = jnp.concatenate(
        [
            expert_weights(after(fwd_routes[0], out), fwd_probs[0]),
            expert_weights(after(bwd_routes[0], out), bwd_probs[0]),
        ]
    )
    even, odd = by_section(weights, swap_cores(weights), core)
    far = to_next_chips(odd[:2], even[2:], 0)
    weights = jnp.concatenate([even[:2], far[:2], odd[2:], far[2:]]).T[:, None]
    weights = jnp.broadcast_to(weights, (GROUPS, shards, 8)).reshape(ranks, 8, 1)

    total = jnp.sum(back.astype(F32) * weights, axis=0).astype(BF16)
    first = jnp.concatenate([total[2:4], total[4:6]])
    second = jnp.concatenate([total[:2], total[6:]])
    own = jnp.where(core == 0, first, second)
    other = swap_cores(jnp.where(core == 0, second, first))
    whole = jnp.where(
        core == 0,
        jnp.concatenate([own, other], axis=1),
        jnp.concatenate([other, own], axis=1),
    )
    return (whole[None, :2], whole[None, 2:])


def solution(mesh):
    return jax.shard_map(
        local,
        mesh=mesh,
        in_specs=(
            P("section", "expert", None),
            P("section", "expert", None),
            P("section", "expert", None),
            P("section", "expert", None),
            P("section", "expert", None),
            P("section", "expert", None),
            P("section", "expert", None),
            P(None, "expert"),
            P(None, "expert"),
            P("expert", None),
        ),
        out_specs=(P("section", "expert", None), P("section", "expert", None)),
        check_vma=False,
    )
```

```python
import functools
import typing

import jax
import jax.numpy as jnp
from jax import lax
from jax.experimental import pallas as pl
from jax.experimental.pallas import tpu as pltpu
from jax.sharding import PartitionSpec as P

GROUPS = 4
PARTS = 4
BATCH = 8
F32 = jnp.float32
BF16 = jnp.bfloat16


def swap_cores(block):
    sections = range(lax.axis_size("section"))
    return lax.ppermute(block, "section", [(i, i ^ 1) for i in sections])


def expert_weights(routes, probs):
    named = routes[:, :, None] == jnp.arange(GROUPS, dtype=jnp.int32)
    return jnp.sum(jnp.where(named, probs[:, :, None], 0.0), axis=1)


def by_section(mine, theirs, core):
    return jnp.where(core == 0, mine, theirs), jnp.where(core == 0, theirs, mine)


def swap_ranks(block, bit):
    ranks = range(lax.axis_size("expert"))
    return lax.ppermute(block, "expert", [(i, i ^ bit) for i in ranks])


def to_next_chips(fwd, bwd, bit):
    sections, ranks = lax.axis_size("section"), lax.axis_size("expert")

    def move(block, pairs):
        route = [(a * ranks + e, b * ranks + (e ^ bit)) for a, b in pairs for e in range(ranks)]
        return lax.ppermute(block, ("section", "expert"), route)

    up = [(i, i + 2) for i in range(sections - 2)]
    down = [(b, a) for a, b in up]
    if sections != 4:
        return [move(fwd, up), move(bwd, down)]
    return [move(jnp.where(lax.axis_index("section") < 2, fwd, bwd), up + down)]


def folded(block):
    rows, width = block.shape
    block = block.reshape(rows, PARTS, width // PARTS).transpose(1, 0, 2)
    return block.reshape(rows * PARTS, width // PARTS)


def unfolded(block):
    rows, width = block.shape
    block = block.reshape(PARTS, rows // PARTS, width).transpose(1, 0, 2)
    return block.reshape(rows // PARTS, width * PARTS)


class Plan(typing.NamedTuple):
    fwd: int
    both: int
    bwd: int
    rows: int
    places: tuple
    other: tuple


def plan_of(sections):
    if sections == 4:
        places = ((0, 2, 0), (24, 4, 0), (8, 4, 0), (24, 4, 2), (8, 4, 2))
        other = (None, (24, 2, 0), None, (32, 2, 0), None)
        return Plan(1, 1, 1, 40, places, other)
    places = ((0, 2, 0), (24, 2, 0), (8, 4, 0), (32, 4, 0), (8, 4, 2), (32, 4, 2))
    return Plan(2, 0, 2, 48, places, (None,) * 6)


def dot(a, b):
    return jnp.dot(a, b, preferred_element_type=F32)


def one_hot(rows, want):
    out = lax.broadcasted_iota(jnp.int32, (rows, rows), 0)
    src = lax.broadcasted_iota(jnp.int32, (rows, rows), 1)
    return jnp.where(want(out) == src, 1.0, 0.0).astype(BF16)


def gathered_order(plan, forward):
    kinds = len(plan.places)

    def want(out):
        part, rest = lax.div(out, kinds * 2 * BATCH), lax.rem(out, kinds * 2 * BATCH)
        kind, rest = lax.div(rest, 2 * BATCH), lax.rem(rest, 2 * BATCH)
        row = jnp.zeros_like(out)
        for i, (here, there) in enumerate(zip(plan.places, plan.other, strict=True)):
            base, size, offset = here
            if there is not None:
                base, size, offset = (
                    jnp.where(forward == 1, t, h) for h, t in zip(here, there, strict=True)
                )
            row = jnp.where(kind == i, base + offset + part * size, row)
        return lax.div(rest, 2) * plan.rows + row + lax.rem(rest, 2)

    return one_hot(BATCH * plan.rows, want)


def returned_order(groups):
    size = PARTS * groups * 2

    def want(out):
        block, rest = lax.div(out, size), lax.rem(out, size)
        return lax.div(rest, 2) * (2 * BATCH) + block * 2 + lax.rem(rest, 2)

    return one_hot(BATCH * size, want)


def fetch_kernel(steps, axis, order, place, weight, earlier, held, turned, zero, *rest):
    sems = rest[-1]
    size = held.shape[axis] // steps
    base = place[0] * held.shape[axis]

    def at(start):
        rows = pl.ds(pl.multiple_of(start, 128), size)
        return rows if axis == 0 else (slice(None), rows)

    copies = [
        pltpu.make_async_copy(
            weight.at[at(base + i * size)], held.at[at(i * size)], sems.at[i]
        )
        for i in range(steps)
    ]
    for copy in copies:
        copy.start()
    if order is not None:
        rest[0][...] = order(place)
    for i, copy in enumerate(copies):
        copy.wait()
        here = slice(i * size, (i + 1) * size)
        if axis == 0:
            turned[:, here] = held[here, :].T
        else:
            turned[here, :] = held[:, here].T
    zero[...] = jnp.zeros_like(zero)


def fetch(place, weight, axis, earlier, like, order=None, count=0):
    steps = 4
    shape = list(weight.shape)
    shape[axis] //= 2
    return pl.pallas_call(
        functools.partial(fetch_kernel, steps, axis, order),
        in_specs=[
            pl.BlockSpec(memory_space=pltpu.SMEM),
            pl.BlockSpec(memory_space=pltpu.HBM),
            pl.BlockSpec(memory_space=pl.ANY),
        ],
        out_specs=[pl.BlockSpec(memory_space=pltpu.VMEM)] * (3 + (count > 0)),
        out_shape=[
            pltpu.VMEM(tuple(shape), BF16),
            pltpu.VMEM(tuple(shape[::-1]), BF16),
            jax.ShapeDtypeStruct(like, BF16),
            pltpu.VMEM((count, count), BF16),
        ][: 3 + (count > 0)],
        scratch_shapes=[pltpu.SemaphoreType.DMA((steps,))],
        compiler_params=pltpu.CompilerParams(vmem_limit_bytes=2**21),
        cost_estimate=pl.CostEstimate(
            flops=0, bytes_accessed=weight.size * 4, transcendentals=0
        ),
    )(place, pltpu.with_memory_space_constraint(weight, pltpu.HBM), earlier)


def up_kernel(plan, ranks, order, first, second, third, fourth, g, u, d_t, out):
    hid = g.shape[1]
    n = 2 * BATCH
    kinds = len(plan.places)
    groups = plan.fwd + plan.both + plan.bwd
    piece = first.shape[1]
    blocks = jnp.concatenate([first[...], second[...], third[...], fourth[...]])
    order = order[...]
    count = order.shape[0]
    batches = ranks // BATCH
    sorted_rows = [
        dot(order, blocks[i * count : (i + 1) * count]).astype(BF16) for i in range(batches)
    ]
    a, b, dh = 0.0, 0.0, 0.0
    for part in range(PARTS):
        cols = slice(part * piece, (part + 1) * piece)
        at = [(part * kinds + kind) * n for kind in range(kinds)]
        taken = [jnp.concatenate([rows[i : i + n] for rows in sorted_rows]) for i in at]
        rows = jnp.concatenate(taken[:groups])
        a += dot(rows, g[cols, :])
        b += dot(rows, u[cols, :])
        dh += dot(jnp.concatenate(taken[groups:]), d_t[cols, :])
    n = n * batches
    for i in range(groups):
        out[:, i * hid : (i + 1) * hid] = a[i * n : (i + 1) * n]
        out[:, (groups + i) * hid : (groups + i + 1) * hid] = b[i * n : (i + 1) * n]
    for i in range(kinds - groups):
        at = (2 * groups + i) * hid
        out[:, at : at + hid] = dh[i * n : (i + 1) * n]


def down_kernel(plan, ranks, place, order, mine, theirs, g_t, u_t, d, kept, sent):
    hid = d.shape[0]
    groups = plan.fwd + plan.both + plan.bwd
    n = 2 * ranks
    split = plan.fwd * n

    def summed(i):
        return mine[:, i * hid : (i + 1) * hid] + theirs[:, i * hid : (i + 1) * hid]

    h, da, du = [], [], []
    forward = jnp.where(place[2] == 1, 1.0, 0.0)
    for i in range(groups):
        a, b = summed(i), summed(groups + i)
        s = jax.nn.sigmoid(a)
        if i < plan.fwd + plan.both:
            hidden = (a * s * b).astype(BF16)
            h.append(hidden if i < plan.fwd else hidden * forward.astype(BF16))
        if i >= plan.fwd:
            dh = summed(2 * groups + i - plan.fwd)
            da.append((dh * b * s * (1.0 + a * (1.0 - s))).astype(BF16))
            du.append((dh * a * s).astype(BF16))
    h, da, du = jnp.concatenate(h), jnp.concatenate(da), jnp.concatenate(du)
    piece = kept.shape[1]
    results = []
    for part in range(PARTS):
        cols = slice(part * piece, (part + 1) * piece)
        y = dot(h, d[:, cols])
        dx = dot(da, g_t[:, cols]) + dot(du, u_t[:, cols])
        shared = plan.both * n
        rows = [y[:split], y[split:] + dx[:shared], dx[shared:]] if shared else [y, dx]
        results.append(jnp.concatenate(rows).astype(BF16))
    order = order[...]
    size = 2 * BATCH
    rows = [
        jnp.concatenate(
            [
                result[i * n + batch * size : i * n + (batch + 1) * size]
                for result in results
                for i in range(groups)
            ]
        )
        for batch in range(ranks // BATCH)
    ]
    rows = jnp.concatenate([dot(order, batch).astype(BF16) for batch in rows])
    kept[...] = rows[: kept.shape[0]]
    sent[...] = rows[kept.shape[0] :]


def pair_kernel(kept, got, weights, *pairs):
    size = pairs[0].shape[0]
    for i, pair in enumerate(pairs):
        rows = slice(i * size, (i + 1) * size)
        pair[...] = (kept[rows].astype(F32) + got[rows].astype(F32)).astype(BF16)


def finish_kernel(plan, offsets, shards, ranks, place, weights, *refs):
    *back, own, other = refs
    total = 0.0
    for offset, block in zip(offsets, back, strict=True):
        expert = lax.div(lax.bitwise_xor(place[1], jnp.int32(offset)), jnp.int32(shards))
        named = lax.broadcasted_iota(jnp.int32, weights.shape, 1) == expert
        weight = jnp.sum(jnp.where(named, weights[...], 0.0), axis=1, keepdims=True)
        total += block[...].astype(F32) * weight
    forward = jnp.where(place[2] == 1, 1.0, 0.0)
    size = 2 * (plan.fwd + plan.both + plan.bwd)
    even, odd = [], []
    for part in range(PARTS):
        rows = [total[i : i + 2] for i in range(part * size, (part + 1) * size, 2)]
        if plan.both:
            fwd, far, bwd = rows
            even += [far * forward, bwd]
            odd += [fwd, far * (1.0 - forward)]
        else:
            fwd, far_fwd, bwd, far_bwd = rows
            even += [far_fwd, bwd]
            odd += [fwd, far_bwd]
    even, odd = jnp.concatenate(even), jnp.concatenate(odd)
    own[...] = jnp.where(place[0] == 0, even, odd).astype(BF16)
    other[...] = jnp.where(place[0] == 0, odd, even).astype(BF16)


def on_core(kernel, place, operands, results, cost):
    specs = [pl.BlockSpec(memory_space=pltpu.VMEM)] * len(operands)
    operands = [pltpu.with_memory_space_constraint(x, pltpu.VMEM) for x in operands]
    if place is not None:
        specs = [pl.BlockSpec(memory_space=pltpu.SMEM)] + specs
        operands = [place] + operands
    ranks = lax.axis_size("expert")
    return pl.pallas_call(
        kernel,
        in_specs=specs,
        out_specs=[pl.BlockSpec(memory_space=pltpu.VMEM)] * len(results),
        out_shape=[jax.ShapeDtypeStruct(*result) for result in results],
        compiler_params=pltpu.CompilerParams(vmem_limit_bytes=ranks * 3 * 2**17),
        cost_estimate=pl.CostEstimate(
            flops=cost * 512, bytes_accessed=cost * 2, transcendentals=0
        ),
    )(*operands)


def after(value, other):
    return lax.optimization_barrier((value, other))[0]


def local(
    fwd_tokens,
    fwd_routes,
    fwd_probs,
    bwd_tokens,
    bwd_routes,
    bwd_probs,
    bwd_grads,
    w_gate,
    w_up,
    w_down,
):
    ranks, sections = lax.axis_size("expert"), lax.axis_size("section")
    shards = ranks // GROUPS
    plan = plan_of(sections)
    groups = plan.fwd + plan.both + plan.bwd
    width = fwd_tokens.shape[2]
    half = width // 2
    hid = w_gate.shape[1]
    section = lax.axis_index("section")
    core = section % 2
    place = jnp.stack([core, lax.axis_index("expert"), section >= 2]).astype(jnp.int32)

    rows = jnp.concatenate([fwd_tokens[0], bwd_tokens[0], bwd_grads[0]])
    keep, send = by_section(rows[:, :half], rows[:, half:], core)
    even, odd = by_section(keep, swap_cores(send), core)

    near = jnp.concatenate([folded(even[:2]), folded(odd[2:])])
    far_fwd, far_bwd = folded(odd[:2]), folded(even[2:])
    if plan.both:
        far_fwd = jnp.pad(far_fwd, ((0, far_bwd.shape[0] - far_fwd.shape[0]), (0, 0)))
    top = ranks // 2
    far = to_next_chips(far_fwd, far_bwd, 0)
    far_top = to_next_chips(far_fwd, far_bwd, top)
    blocks = jnp.concatenate([near, *far, swap_ranks(near, top), *far_top])
    offsets = [0, top]
    g, g_t, zero = fetch(place, w_gate, 0, near, blocks.shape)
    blocks = blocks + zero
    bit = top // 2
    while bit > 2:
        blocks = jnp.concatenate([blocks, swap_ranks(blocks, bit)])
        offsets += [o ^ bit for o in offsets]
        bit //= 2
    offsets += [o ^ 2 for o in offsets]
    second = swap_ranks(blocks, 2)
    third = swap_ranks(blocks, 1)
    u, u_t, zero, back_order = fetch(
        place,
        w_up,
        0,
        blocks,
        second.shape,
        lambda _: returned_order(groups),
        BATCH * PARTS * groups * 2,
    )
    second = second + zero
    fourth = swap_ranks(second, 1)
    d, d_t, _, got_order = fetch(
        place,
        w_down,
        1,
        second,
        (16, 128),
        lambda place: gathered_order(plan, place[2]),
        BATCH * plan.rows,
    )

    (mine,) = on_core(
        functools.partial(up_kernel, plan, ranks),
        None,
        (got_order, blocks, second, third, fourth, g, u, d_t),
        [((2 * ranks, (groups + len(plan.places)) * hid), F32)],
        3 * hid * half,
    )
    kept, sent = on_core(
        functools.partial(down_kernel, plan, ranks),
        place,
        (back_order, mine, swap_cores(mine), g_t, u_t, d),
        [((ranks // 2 * PARTS * groups * 2, half // PARTS), BF16)] * 2,
        3 * hid * half,
    )
    weights = jnp.concatenate(
        [
            expert_weights(after(fwd_routes[0], sent), fwd_probs[0]),
            expert_weights(after(bwd_routes[0], sent), bwd_probs[0]),
        ]
    )
    even, odd = by_section(weights, swap_cores(weights), core)
    far = to_next_chips(odd[:2], even[2:], 0)
    weights = jnp.concatenate([even[:2], far[0], odd[2:], *far[1:]])
    weights = jnp.concatenate([weights] * PARTS)
    block = ((PARTS * groups * 2, half // PARTS), BF16)
    pairs = on_core(
        pair_kernel, None, (kept, swap_ranks(sent, 1), weights), [block] * (ranks // 2), half
    )
    back = [swap_ranks(pair, o) if o else pair for pair, o in zip(pairs, offsets, strict=True)]
    own, other = on_core(
        functools.partial(finish_kernel, plan, offsets, shards, ranks),
        place,
        (weights, *back),
        [((4 * PARTS, half // PARTS), BF16)] * 2,
        half,
    )
    own, other = unfolded(own), unfolded(swap_cores(other))
    whole = jnp.where(
        core == 0,
        jnp.concatenate([own, other], axis=1),
        jnp.concatenate([other, own], axis=1),
    )
    return (whole[None, :2], whole[None, 2:])


def solution(mesh):
    return jax.shard_map(
        local,
        mesh=mesh,
        in_specs=(
            P("section", "expert", None),
            P("section", "expert", None),
            P("section", "expert", None),
            P("section", "expert", None),
            P("section", "expert", None),
            P("section", "expert", None),
            P("section", "expert", None),
            P(None, "expert"),
            P(None, "expert"),
            P("expert", None),
        ),
        out_specs=(P("section", "expert", None), P("section", "expert", None)),
        check_vma=False,
    )
```

```python
import functools
import typing

import jax
import jax.numpy as jnp
from jax import lax
from jax.experimental import pallas as pl
from jax.experimental.pallas import tpu as pltpu
from jax.sharding import PartitionSpec as P

GROUPS = 4
PARTS = 4
BATCH = 8
F32 = jnp.float32
BF16 = jnp.bfloat16


def swap_cores(block):
    sections = range(lax.axis_size("section"))
    return lax.ppermute(block, "section", [(i, i ^ 1) for i in sections])


def expert_weights(routes, probs):
    named = routes[:, :, None] == jnp.arange(GROUPS, dtype=jnp.int32)
    return jnp.sum(jnp.where(named, probs[:, :, None], 0.0), axis=1)


def by_section(mine, theirs, core):
    return jnp.where(core == 0, mine, theirs), jnp.where(core == 0, theirs, mine)


def swap_ranks(block, bit):
    ranks = range(lax.axis_size("expert"))
    return lax.ppermute(block, "expert", [(i, i ^ bit) for i in ranks])


def to_next_chips(fwd, bwd, bit):
    sections, ranks = lax.axis_size("section"), lax.axis_size("expert")

    def move(block, pairs):
        route = [(a * ranks + e, b * ranks + (e ^ bit)) for a, b in pairs for e in range(ranks)]
        return lax.ppermute(block, ("section", "expert"), route)

    up = [(i, i + 2) for i in range(sections - 2)]
    down = [(b, a) for a, b in up]
    if sections != 4:
        return [move(fwd, up), move(bwd, down)]
    return [move(jnp.where(lax.axis_index("section") < 2, fwd, bwd), up + down)]


def folded(block):
    rows, width = block.shape
    block = block.reshape(rows, PARTS, width // PARTS).transpose(1, 0, 2)
    return block.reshape(rows * PARTS, width // PARTS)


def unfolded(block):
    rows, width = block.shape
    block = block.reshape(PARTS, rows // PARTS, width).transpose(1, 0, 2)
    return block.reshape(rows // PARTS, width * PARTS)


class Plan(typing.NamedTuple):
    fwd: int
    both: int
    bwd: int
    rows: int
    places: tuple
    other: tuple


def plan_of(sections):
    if sections == 4:
        places = ((0, 2, 0), (24, 4, 0), (8, 4, 0), (24, 4, 2), (8, 4, 2))
        other = (None, (24, 2, 0), None, (32, 2, 0), None)
        return Plan(1, 1, 1, 40, places, other)
    places = ((0, 2, 0), (24, 2, 0), (8, 4, 0), (32, 4, 0), (8, 4, 2), (32, 4, 2))
    return Plan(2, 0, 2, 48, places, (None,) * 6)


def dot(a, b):
    return jnp.dot(a, b, preferred_element_type=F32)


def one_hot(rows, want):
    out = lax.broadcasted_iota(jnp.int32, (rows, rows), 0)
    src = lax.broadcasted_iota(jnp.int32, (rows, rows), 1)
    return jnp.where(want(out) == src, 1.0, 0.0).astype(BF16)


def gathered_order(plan, forward):
    kinds = len(plan.places)

    def want(out):
        part, rest = lax.div(out, kinds * 2 * BATCH), lax.rem(out, kinds * 2 * BATCH)
        kind, rest = lax.div(rest, 2 * BATCH), lax.rem(rest, 2 * BATCH)
        row = jnp.zeros_like(out)
        for i, (here, there) in enumerate(zip(plan.places, plan.other, strict=True)):
            base, size, offset = here
            if there is not None:
                base, size, offset = (
                    jnp.where(forward == 1, t, h) for h, t in zip(here, there, strict=True)
                )
            row = jnp.where(kind == i, base + offset + part * size, row)
        return lax.div(rest, 2) * plan.rows + row + lax.rem(rest, 2)

    return one_hot(BATCH * plan.rows, want)


def returned_order(groups):
    size = PARTS * groups * 2

    def want(out):
        block, rest = lax.div(out, size), lax.rem(out, size)
        return lax.div(rest, 2) * (2 * BATCH) + block * 2 + lax.rem(rest, 2)

    return one_hot(BATCH * size, want)


class Piece(typing.NamedTuple):
    weight: int
    axis: int
    start: int
    size: int
    steps: int


def fetch_kernel(pieces, order, place, *refs):
    count = 1 + max(piece.weight for piece in pieces)
    weights, refs = refs[:count], refs[count + 1 :]
    *outs, zero, made, sems = refs
    copies = []
    for i, piece in enumerate(pieces):
        weight, held = weights[piece.weight], outs[2 * i]
        half = weight.shape[piece.axis] // 2
        size = piece.size // piece.steps
        for step in range(piece.steps):
            start = place[0] * half + piece.start + step * size
            there = pl.ds(pl.multiple_of(start, 128), size)
            here = pl.ds(step * size, size)
            if piece.axis == 1:
                there, here = (slice(None), there), (slice(None), here)
            sem = sems.at[len(copies)]
            copies.append(pltpu.make_async_copy(weight.at[there], held.at[here], sem))
    for copy in copies:
        copy.start()
    zero[...] = jnp.zeros_like(zero)
    made[...] = order(place)
    copies = iter(copies)
    for i, piece in enumerate(pieces):
        held, turned = outs[2 * i : 2 * i + 2]
        size = piece.size // piece.steps
        for step in range(piece.steps):
            next(copies).wait()
            here = slice(step * size, (step + 1) * size)
            if piece.axis == 0:
                turned[:, here] = held[here, :].T
            else:
                turned[here, :] = held[:, here].T


def fetch(place, weights, pieces, earlier, like, order, count):
    shapes = []
    for piece in pieces:
        shape = list(weights[piece.weight].shape)
        shape[piece.axis] = piece.size
        shapes += [tuple(shape), tuple(shape[::-1])]
    nbytes = sum(piece.size for piece in pieces) * weights[0].shape[1] * 4
    steps = sum(piece.steps for piece in pieces)
    return pl.pallas_call(
        functools.partial(fetch_kernel, pieces, order),
        in_specs=[pl.BlockSpec(memory_space=pltpu.SMEM)]
        + [pl.BlockSpec(memory_space=pltpu.HBM)] * len(weights)
        + [pl.BlockSpec(memory_space=pl.ANY)],
        out_specs=[pl.BlockSpec(memory_space=pltpu.VMEM)] * (len(shapes) + 2),
        out_shape=[pltpu.VMEM(shape, BF16) for shape in shapes]
        + [jax.ShapeDtypeStruct(like, BF16), pltpu.VMEM((count, count), BF16)],
        scratch_shapes=[pltpu.SemaphoreType.DMA((steps,))],
        compiler_params=pltpu.CompilerParams(vmem_limit_bytes=2**21),
        cost_estimate=pl.CostEstimate(flops=0, bytes_accessed=nbytes, transcendentals=0),
    )(
        place,
        *[pltpu.with_memory_space_constraint(weight, pltpu.HBM) for weight in weights],
        earlier,
    )


def up_kernel(plan, ranks, order, first, second, third, fourth, g, u_low, u_high, d_t, out):
    hid = g.shape[1]
    n = 2 * BATCH
    kinds = len(plan.places)
    groups = plan.fwd + plan.both + plan.bwd
    piece = first.shape[1]
    blocks = jnp.concatenate([first[...], second[...], third[...], fourth[...]])
    order = order[...]
    count = order.shape[0]
    batches = ranks // BATCH
    sorted_rows = [
        dot(order, blocks[i * count : (i + 1) * count]).astype(BF16) for i in range(batches)
    ]
    a, b, dh = 0.0, 0.0, 0.0
    for part in range(PARTS):
        cols = slice(part * piece, (part + 1) * piece)
        at = [(part * kinds + kind) * n for kind in range(kinds)]
        taken = [jnp.concatenate([rows[i : i + n] for rows in sorted_rows]) for i in at]
        rows = jnp.concatenate(taken[:groups])
        a += dot(rows, g[cols, :])
        u = u_high[(part - 1) * piece : part * piece, :] if part else u_low[...]
        b += dot(rows, u)
        dh += dot(jnp.concatenate(taken[groups:]), d_t[cols, :])
    n = n * batches
    for i in range(groups):
        out[:, i * hid : (i + 1) * hid] = a[i * n : (i + 1) * n]
        out[:, (groups + i) * hid : (groups + i + 1) * hid] = b[i * n : (i + 1) * n]
    for i in range(kinds - groups):
        at = (2 * groups + i) * hid
        out[:, at : at + hid] = dh[i * n : (i + 1) * n]


def down_kernel(plan, ranks, place, order, mine, theirs, g_t, u_t_low, u_t_high, d, kept, sent):
    hid = d.shape[0]
    groups = plan.fwd + plan.both + plan.bwd
    n = 2 * ranks
    split = plan.fwd * n

    def summed(i):
        return mine[:, i * hid : (i + 1) * hid] + theirs[:, i * hid : (i + 1) * hid]

    h, da, du = [], [], []
    forward = jnp.where(place[2] == 1, 1.0, 0.0)
    for i in range(groups):
        a, b = summed(i), summed(groups + i)
        s = jax.nn.sigmoid(a)
        if i < plan.fwd + plan.both:
            hidden = (a * s * b).astype(BF16)
            h.append(hidden if i < plan.fwd else hidden * forward.astype(BF16))
        if i >= plan.fwd:
            dh = summed(2 * groups + i - plan.fwd)
            da.append((dh * b * s * (1.0 + a * (1.0 - s))).astype(BF16))
            du.append((dh * a * s).astype(BF16))
    h, da, du = jnp.concatenate(h), jnp.concatenate(da), jnp.concatenate(du)
    piece = kept.shape[1]
    results = []
    for part in range(PARTS):
        cols = slice(part * piece, (part + 1) * piece)
        y = dot(h, d[:, cols])
        u_t = u_t_high[:, (part - 1) * piece : part * piece] if part else u_t_low[...]
        dx = dot(da, g_t[:, cols]) + dot(du, u_t)
        shared = plan.both * n
        rows = [y[:split], y[split:] + dx[:shared], dx[shared:]] if shared else [y, dx]
        results.append(jnp.concatenate(rows).astype(BF16))
    order = order[...]
    size = 2 * BATCH
    rows = [
        jnp.concatenate(
            [
                result[i * n + batch * size : i * n + (batch + 1) * size]
                for result in results
                for i in range(groups)
            ]
        )
        for batch in range(ranks // BATCH)
    ]
    rows = jnp.concatenate([dot(order, batch).astype(BF16) for batch in rows])
    kept[...] = rows[: kept.shape[0]]
    sent[...] = rows[kept.shape[0] :]


def pair_kernel(kept, got, weights, *pairs):
    size = pairs[0].shape[0]
    for i, pair in enumerate(pairs):
        rows = slice(i * size, (i + 1) * size)
        pair[...] = (kept[rows].astype(F32) + got[rows].astype(F32)).astype(BF16)


def finish_kernel(plan, offsets, shards, ranks, place, weights, *refs):
    *back, own, other = refs
    total = 0.0
    for offset, block in zip(offsets, back, strict=True):
        expert = lax.div(lax.bitwise_xor(place[1], jnp.int32(offset)), jnp.int32(shards))
        named = lax.broadcasted_iota(jnp.int32, weights.shape, 1) == expert
        weight = jnp.sum(jnp.where(named, weights[...], 0.0), axis=1, keepdims=True)
        total += block[...].astype(F32) * weight
    forward = jnp.where(place[2] == 1, 1.0, 0.0)
    size = 2 * (plan.fwd + plan.both + plan.bwd)
    even, odd = [], []
    for part in range(PARTS):
        rows = [total[i : i + 2] for i in range(part * size, (part + 1) * size, 2)]
        if plan.both:
            fwd, far, bwd = rows
            even += [far * forward, bwd]
            odd += [fwd, far * (1.0 - forward)]
        else:
            fwd, far_fwd, bwd, far_bwd = rows
            even += [far_fwd, bwd]
            odd += [fwd, far_bwd]
    even, odd = jnp.concatenate(even), jnp.concatenate(odd)
    own[...] = jnp.where(place[0] == 0, even, odd).astype(BF16)
    other[...] = jnp.where(place[0] == 0, odd, even).astype(BF16)


def on_core(kernel, place, operands, results, cost):
    specs = [pl.BlockSpec(memory_space=pltpu.VMEM)] * len(operands)
    operands = [pltpu.with_memory_space_constraint(x, pltpu.VMEM) for x in operands]
    if place is not None:
        specs = [pl.BlockSpec(memory_space=pltpu.SMEM)] + specs
        operands = [place] + operands
    ranks = lax.axis_size("expert")
    return pl.pallas_call(
        kernel,
        in_specs=specs,
        out_specs=[pl.BlockSpec(memory_space=pltpu.VMEM)] * len(results),
        out_shape=[jax.ShapeDtypeStruct(*result) for result in results],
        compiler_params=pltpu.CompilerParams(vmem_limit_bytes=ranks * 3 * 2**17),
        cost_estimate=pl.CostEstimate(
            flops=cost * 512, bytes_accessed=cost * 2, transcendentals=0
        ),
    )(*operands)


def after(value, other):
    return lax.optimization_barrier((value, other))[0]


def local(
    fwd_tokens,
    fwd_routes,
    fwd_probs,
    bwd_tokens,
    bwd_routes,
    bwd_probs,
    bwd_grads,
    w_gate,
    w_up,
    w_down,
):
    ranks, sections = lax.axis_size("expert"), lax.axis_size("section")
    shards = ranks // GROUPS
    plan = plan_of(sections)
    groups = plan.fwd + plan.both + plan.bwd
    width = fwd_tokens.shape[2]
    half = width // 2
    hid = w_gate.shape[1]
    section = lax.axis_index("section")
    core = section % 2
    place = jnp.stack([core, lax.axis_index("expert"), section >= 2]).astype(jnp.int32)

    rows = jnp.concatenate([fwd_tokens[0], bwd_tokens[0], bwd_grads[0]])
    keep, send = by_section(rows[:, :half], rows[:, half:], core)
    even, odd = by_section(keep, swap_cores(send), core)

    near = jnp.concatenate([folded(even[:2]), folded(odd[2:])])
    far_fwd, far_bwd = folded(odd[:2]), folded(even[2:])
    if plan.both:
        far_fwd = jnp.pad(far_fwd, ((0, far_bwd.shape[0] - far_fwd.shape[0]), (0, 0)))
    top = ranks // 2
    far = to_next_chips(far_fwd, far_bwd, 0)
    far_top = to_next_chips(far_fwd, far_bwd, top)
    blocks = jnp.concatenate([near, *far, swap_ranks(near, top), *far_top])
    offsets = [0, top]
    piece = half // PARTS
    g, g_t, u_low, u_t_low, zero, back_order = fetch(
        place,
        (w_gate, w_up),
        (Piece(0, 0, 0, half, 4), Piece(1, 0, 0, piece, 1)),
        near,
        blocks.shape,
        lambda _: returned_order(groups),
        BATCH * PARTS * groups * 2,
    )
    blocks = blocks + zero
    bit = top // 2
    while bit > 2:
        blocks = jnp.concatenate([blocks, swap_ranks(blocks, bit)])
        offsets += [o ^ bit for o in offsets]
        bit //= 2
    offsets += [o ^ 2 for o in offsets]
    fourth = swap_ranks(blocks, 3)
    second = swap_ranks(blocks, 2)
    third = swap_ranks(blocks, 1)
    u_high, u_t_high, d, d_t, _, got_order = fetch(
        place,
        (w_up, w_down),
        (Piece(0, 0, piece, half - piece, 3), Piece(1, 1, 0, half, 4)),
        blocks,
        (16, 128),
        lambda place: gathered_order(plan, place[2]),
        BATCH * plan.rows,
    )

    (mine,) = on_core(
        functools.partial(up_kernel, plan, ranks),
        None,
        (got_order, blocks, second, third, fourth, g, u_low, u_high, d_t),
        [((2 * ranks, (groups + len(plan.places)) * hid), F32)],
        3 * hid * half,
    )
    kept, sent = on_core(
        functools.partial(down_kernel, plan, ranks),
        place,
        (back_order, mine, swap_cores(mine), g_t, u_t_low, u_t_high, d),
        [((ranks // 2 * PARTS * groups * 2, half // PARTS), BF16)] * 2,
        3 * hid * half,
    )
    weights = jnp.concatenate(
        [
            expert_weights(after(fwd_routes[0], sent), fwd_probs[0]),
            expert_weights(after(bwd_routes[0], sent), bwd_probs[0]),
        ]
    )
    even, odd = by_section(weights, swap_cores(weights), core)
    far = to_next_chips(odd[:2], even[2:], 0)
    weights = jnp.concatenate([even[:2], far[0], odd[2:], *far[1:]])
    weights = jnp.concatenate([weights] * PARTS)
    block = ((PARTS * groups * 2, half // PARTS), BF16)
    pairs = on_core(
        pair_kernel, None, (kept, swap_ranks(sent, 1), weights), [block] * (ranks // 2), half
    )
    pairs = dict(zip(offsets, pairs, strict=True))
    offsets = [0] + sorted(offsets[1:], reverse=True)
    back = [swap_ranks(pairs[o], o) if o else pairs[o] for o in offsets]
    own, other = on_core(
        functools.partial(finish_kernel, plan, offsets, shards, ranks),
        place,
        (weights, *back),
        [((4 * PARTS, half // PARTS), BF16)] * 2,
        half,
    )
    own, other = unfolded(own), unfolded(swap_cores(other))
    whole = jnp.where(
        core == 0,
        jnp.concatenate([own, other], axis=1),
        jnp.concatenate([other, own], axis=1),
    )
    return (whole[None, :2], whole[None, 2:])


def solution(mesh):
    return jax.shard_map(
        local,
        mesh=mesh,
        in_specs=(
            P("section", "expert", None),
            P("section", "expert", None),
            P("section", "expert", None),
            P("section", "expert", None),
            P("section", "expert", None),
            P("section", "expert", None),
            P("section", "expert", None),
            P(None, "expert"),
            P(None, "expert"),
            P("expert", None),
        ),
        out_specs=(P("section", "expert", None), P("section", "expert", None)),
        check_vma=False,
    )
```

```python
import functools
import typing

import jax
import jax.numpy as jnp
from jax import lax
from jax.experimental import pallas as pl
from jax.experimental.pallas import tpu as pltpu
from jax.sharding import PartitionSpec as P

GROUPS = 4
PARTS = 4
BATCH = 8
F32 = jnp.float32
BF16 = jnp.bfloat16


def swap_cores(block):
    sections = range(lax.axis_size("section"))
    return lax.ppermute(block, "section", [(i, i ^ 1) for i in sections])


def expert_weights(routes, probs):
    named = routes[:, :, None] == jnp.arange(GROUPS, dtype=jnp.int32)
    return jnp.sum(jnp.where(named, probs[:, :, None], 0.0), axis=1)


def by_section(mine, theirs, core):
    return jnp.where(core == 0, mine, theirs), jnp.where(core == 0, theirs, mine)


def swap_ranks(block, bit):
    ranks = range(lax.axis_size("expert"))
    return lax.ppermute(block, "expert", [(i, i ^ bit) for i in ranks])


def to_next_chips(fwd, bwd, bit):
    sections, ranks = lax.axis_size("section"), lax.axis_size("expert")

    def move(block, pairs):
        route = [(a * ranks + e, b * ranks + (e ^ bit)) for a, b in pairs for e in range(ranks)]
        return lax.ppermute(block, ("section", "expert"), route)

    up = [(i, i + 2) for i in range(sections - 2)]
    down = [(b, a) for a, b in up]
    if sections != 4:
        return [move(fwd, up), move(bwd, down)]
    return [move(jnp.where(lax.axis_index("section") < 2, fwd, bwd), up + down)]


def folded(block):
    rows, width = block.shape
    block = block.reshape(rows, PARTS, width // PARTS).transpose(1, 0, 2)
    return block.reshape(rows * PARTS, width // PARTS)


def unfolded(block):
    rows, width = block.shape
    block = block.reshape(PARTS, rows // PARTS, width).transpose(1, 0, 2)
    return block.reshape(rows // PARTS, width * PARTS)


class Plan(typing.NamedTuple):
    fwd: int
    both: int
    bwd: int
    rows: int
    places: tuple
    other: tuple


def plan_of(sections):
    if sections == 4:
        places = ((0, 2, 0), (24, 4, 0), (8, 4, 0), (24, 4, 2), (8, 4, 2))
        other = (None, (24, 2, 0), None, (32, 2, 0), None)
        return Plan(1, 1, 1, 40, places, other)
    places = ((0, 2, 0), (24, 2, 0), (8, 4, 0), (32, 4, 0), (8, 4, 2), (32, 4, 2))
    return Plan(2, 0, 2, 48, places, (None,) * 6)


def dot(a, b):
    return jnp.dot(a, b, preferred_element_type=F32)


def one_hot(rows, want):
    out = lax.broadcasted_iota(jnp.int32, (rows, rows), 0)
    src = lax.broadcasted_iota(jnp.int32, (rows, rows), 1)
    return jnp.where(want(out) == src, 1.0, 0.0).astype(BF16)


def gathered_order(plan, forward):
    kinds = len(plan.places)

    def want(out):
        part, rest = lax.div(out, kinds * 2 * BATCH), lax.rem(out, kinds * 2 * BATCH)
        kind, rest = lax.div(rest, 2 * BATCH), lax.rem(rest, 2 * BATCH)
        row = jnp.zeros_like(out)
        for i, (here, there) in enumerate(zip(plan.places, plan.other, strict=True)):
            base, size, offset = here
            if there is not None:
                base, size, offset = (
                    jnp.where(forward == 1, t, h) for h, t in zip(here, there, strict=True)
                )
            row = jnp.where(kind == i, base + offset + part * size, row)
        return lax.div(rest, 2) * plan.rows + row + lax.rem(rest, 2)

    return one_hot(BATCH * plan.rows, want)


def returned_order(groups):
    size = PARTS * groups * 2

    def want(out):
        block, rest = lax.div(out, size), lax.rem(out, size)
        return lax.div(rest, 2) * (2 * BATCH) + block * 2 + lax.rem(rest, 2)

    return one_hot(BATCH * size, want)


class Piece(typing.NamedTuple):
    weight: int
    axis: int
    start: int
    size: int
    steps: int


def fetch_kernel(pieces, order, place, *refs):
    count = 1 + max(piece.weight for piece in pieces)
    weights, refs = refs[:count], refs[count + 1 :]
    *outs, zero, made, sems = refs
    copies = []
    for i, piece in enumerate(pieces):
        weight, held = weights[piece.weight], outs[2 * i]
        half = weight.shape[piece.axis] // 2
        size = piece.size // piece.steps
        for step in range(piece.steps):
            start = place[0] * half + piece.start + step * size
            there = pl.ds(pl.multiple_of(start, 128), size)
            here = pl.ds(step * size, size)
            if piece.axis == 1:
                there, here = (slice(None), there), (slice(None), here)
            sem = sems.at[len(copies)]
            copies.append(pltpu.make_async_copy(weight.at[there], held.at[here], sem))
    for copy in copies:
        copy.start()
    zero[...] = jnp.zeros_like(zero)
    made[...] = order(place)
    copies = iter(copies)
    for i, piece in enumerate(pieces):
        held, turned = outs[2 * i : 2 * i + 2]
        size = piece.size // piece.steps
        for step in range(piece.steps):
            next(copies).wait()
            here = slice(step * size, (step + 1) * size)
            if piece.axis == 0:
                turned[:, here] = held[here, :].T
            else:
                turned[here, :] = held[:, here].T


def fetch(place, weights, pieces, earlier, like, order, count):
    shapes = []
    for piece in pieces:
        shape = list(weights[piece.weight].shape)
        shape[piece.axis] = piece.size
        shapes += [tuple(shape), tuple(shape[::-1])]
    nbytes = sum(piece.size for piece in pieces) * weights[0].shape[1] * 4
    steps = sum(piece.steps for piece in pieces)
    return pl.pallas_call(
        functools.partial(fetch_kernel, pieces, order),
        in_specs=[pl.BlockSpec(memory_space=pltpu.SMEM)]
        + [pl.BlockSpec(memory_space=pltpu.HBM)] * len(weights)
        + [pl.BlockSpec(memory_space=pl.ANY)],
        out_specs=[pl.BlockSpec(memory_space=pltpu.VMEM)] * (len(shapes) + 2),
        out_shape=[pltpu.VMEM(shape, BF16) for shape in shapes]
        + [jax.ShapeDtypeStruct(like, BF16), pltpu.VMEM((count, count), BF16)],
        scratch_shapes=[pltpu.SemaphoreType.DMA((steps,))],
        compiler_params=pltpu.CompilerParams(vmem_limit_bytes=2**21),
        cost_estimate=pl.CostEstimate(flops=0, bytes_accessed=nbytes, transcendentals=0),
    )(
        place,
        *[pltpu.with_memory_space_constraint(weight, pltpu.HBM) for weight in weights],
        earlier,
    )


def up_kernel(plan, ranks, order, first, second, third, fourth, g, u_low, u_high, d_t, out):
    hid = g.shape[1]
    n = 2 * BATCH
    kinds = len(plan.places)
    groups = plan.fwd + plan.both + plan.bwd
    piece = first.shape[1]
    blocks = jnp.concatenate([first[...], second[...], third[...], fourth[...]])
    order = order[...]
    count = order.shape[0]
    batches = ranks // BATCH
    sorted_rows = [
        dot(order, blocks[i * count : (i + 1) * count]).astype(BF16) for i in range(batches)
    ]
    a, b, dh = 0.0, 0.0, 0.0
    for part in range(PARTS):
        cols = slice(part * piece, (part + 1) * piece)
        at = [(part * kinds + kind) * n for kind in range(kinds)]
        taken = [jnp.concatenate([rows[i : i + n] for rows in sorted_rows]) for i in at]
        rows = jnp.concatenate(taken[:groups])
        a += dot(rows, g[cols, :])
        u = u_high[(part - 1) * piece : part * piece, :] if part else u_low[...]
        b += dot(rows, u)
        dh += dot(jnp.concatenate(taken[groups:]), d_t[cols, :])
    n = n * batches
    for i in range(groups):
        out[:, i * hid : (i + 1) * hid] = a[i * n : (i + 1) * n]
        out[:, (groups + i) * hid : (groups + i + 1) * hid] = b[i * n : (i + 1) * n]
    for i in range(kinds - groups):
        at = (2 * groups + i) * hid
        out[:, at : at + hid] = dh[i * n : (i + 1) * n]


def down_kernel(plan, ranks, place, order, mine, theirs, g_t, u_t_low, u_t_high, d, kept, sent):
    hid = d.shape[0]
    groups = plan.fwd + plan.both + plan.bwd
    n = 2 * ranks
    split = plan.fwd * n

    def summed(i):
        return mine[:, i * hid : (i + 1) * hid] + theirs[:, i * hid : (i + 1) * hid]

    h, da, du = [], [], []
    forward = jnp.where(place[2] == 1, 1.0, 0.0)
    for i in range(groups):
        a, b = summed(i), summed(groups + i)
        s = jax.nn.sigmoid(a)
        if i < plan.fwd + plan.both:
            hidden = (a * s * b).astype(BF16)
            h.append(hidden if i < plan.fwd else hidden * forward.astype(BF16))
        if i >= plan.fwd:
            dh = summed(2 * groups + i - plan.fwd)
            da.append((dh * b * s * (1.0 + a * (1.0 - s))).astype(BF16))
            du.append((dh * a * s).astype(BF16))
    h, da, du = jnp.concatenate(h), jnp.concatenate(da), jnp.concatenate(du)
    piece = kept.shape[1]
    results = []
    for part in range(PARTS):
        cols = slice(part * piece, (part + 1) * piece)
        y = dot(h, d[:, cols])
        u_t = u_t_high[:, (part - 1) * piece : part * piece] if part else u_t_low[...]
        dx = dot(da, g_t[:, cols]) + dot(du, u_t)
        shared = plan.both * n
        rows = [y[:split], y[split:] + dx[:shared], dx[shared:]] if shared else [y, dx]
        results.append(jnp.concatenate(rows).astype(BF16))
    order = order[...]
    size = 2 * BATCH
    rows = [
        jnp.concatenate(
            [
                result[i * n + batch * size : i * n + (batch + 1) * size]
                for result in results
                for i in range(groups)
            ]
        )
        for batch in range(ranks // BATCH)
    ]
    rows = jnp.concatenate([dot(order, batch).astype(BF16) for batch in rows])
    kept[...] = rows[: kept.shape[0]]
    sent[...] = rows[kept.shape[0] :]


def pair_kernel(kept, got, weights, *pairs):
    size = pairs[0].shape[0]
    for i, pair in enumerate(pairs):
        rows = slice(i * size, (i + 1) * size)
        pair[...] = (kept[rows].astype(F32) + got[rows].astype(F32)).astype(BF16)


def select_kernel(plan, offsets, shards, place, weights, columns, chosen):
    size = weights.shape[0]
    for i, offset in enumerate(offsets):
        expert = lax.div(lax.bitwise_xor(place[1], jnp.int32(offset)), jnp.int32(shards))
        named = lax.broadcasted_iota(jnp.int32, weights.shape, 1) == expert
        weight = jnp.sum(jnp.where(named, weights[...], 0.0), axis=1, keepdims=True)
        columns[i * size : (i + 1) * size, :] = jnp.broadcast_to(weight, (size, 128))
    out = lax.broadcasted_iota(jnp.int32, chosen.shape, 0)
    src = lax.broadcasted_iota(jnp.int32, chosen.shape, 1)
    odd = jnp.where(out < 4 * PARTS, place[0], 1 - place[0])
    part, row = lax.rem(lax.div(out, 4), PARTS), lax.rem(out, 4)
    bwd = lax.div(row, 2)
    if plan.both:
        far = jnp.where(place[2] == 1, 0, 1)
        group = jnp.where(bwd == odd, 1, 2 * bwd)
        present = (bwd != odd) | (bwd == far)
    else:
        group = 2 * bwd + jnp.where(bwd == odd, 1, 0)
        present = out >= 0
    groups = plan.fwd + plan.both + plan.bwd
    want = part * (2 * groups) + group * 2 + lax.rem(row, 2)
    chosen[...] = jnp.where((want == src) & present, 1.0, 0.0).astype(BF16)


def finish_kernel(columns, chosen, *refs):
    *back, own, other = refs
    size = back[0].shape[0]
    total = 0.0
    for i, block in enumerate(back):
        total += block[...].astype(F32) * columns[i * size : (i + 1) * size, :1]
    rows = dot(chosen[...], total.astype(BF16)).astype(BF16)
    own[...] = rows[: own.shape[0]]
    other[...] = rows[own.shape[0] :]


def on_core(kernel, place, operands, results, cost):
    specs = [pl.BlockSpec(memory_space=pltpu.VMEM)] * len(operands)
    operands = [pltpu.with_memory_space_constraint(x, pltpu.VMEM) for x in operands]
    if place is not None:
        specs = [pl.BlockSpec(memory_space=pltpu.SMEM)] + specs
        operands = [place] + operands
    ranks = lax.axis_size("expert")
    return pl.pallas_call(
        kernel,
        in_specs=specs,
        out_specs=[pl.BlockSpec(memory_space=pltpu.VMEM)] * len(results),
        out_shape=[jax.ShapeDtypeStruct(*result) for result in results],
        compiler_params=pltpu.CompilerParams(vmem_limit_bytes=ranks * 3 * 2**17),
        cost_estimate=pl.CostEstimate(
            flops=cost * 512, bytes_accessed=cost * 2, transcendentals=0
        ),
    )(*operands)


def after(value, other):
    return lax.optimization_barrier((value, other))[0]


def local(
    fwd_tokens,
    fwd_routes,
    fwd_probs,
    bwd_tokens,
    bwd_routes,
    bwd_probs,
    bwd_grads,
    w_gate,
    w_up,
    w_down,
):
    ranks, sections = lax.axis_size("expert"), lax.axis_size("section")
    shards = ranks // GROUPS
    plan = plan_of(sections)
    groups = plan.fwd + plan.both + plan.bwd
    width = fwd_tokens.shape[2]
    half = width // 2
    hid = w_gate.shape[1]
    section = lax.axis_index("section")
    core = section % 2
    place = jnp.stack([core, lax.axis_index("expert"), section >= 2]).astype(jnp.int32)

    inputs = [fwd_tokens[0], bwd_tokens[0], bwd_grads[0]]
    theirs = jnp.concatenate([swap_cores(block) for block in inputs])
    mine = jnp.concatenate(inputs)
    mine, theirs = (
        jnp.where(core == 0, rows[:, :half], rows[:, half:]) for rows in (mine, theirs)
    )
    even, odd = by_section(mine, theirs, core)

    near = jnp.concatenate([folded(even[:2]), folded(odd[2:])])
    far_fwd, far_bwd = folded(odd[:2]), folded(even[2:])
    if plan.both:
        far_fwd = jnp.pad(far_fwd, ((0, far_bwd.shape[0] - far_fwd.shape[0]), (0, 0)))
    top = ranks // 2
    far = to_next_chips(far_fwd, far_bwd, 0)
    far_top = to_next_chips(far_fwd, far_bwd, top)
    blocks = jnp.concatenate([near, *far, swap_ranks(near, top), *far_top])
    offsets = [0, top]
    piece = half // PARTS
    g, g_t, u_low, u_t_low, zero, back_order = fetch(
        place,
        (w_gate, w_up),
        (Piece(0, 0, 0, half, 4), Piece(1, 0, 0, piece, 1)),
        near,
        blocks.shape,
        lambda _: returned_order(groups),
        BATCH * PARTS * groups * 2,
    )
    blocks = blocks + zero
    bit = top // 2
    while bit > 2:
        blocks = jnp.concatenate([blocks, swap_ranks(blocks, bit)])
        offsets += [o ^ bit for o in offsets]
        bit //= 2
    offsets += [o ^ 2 for o in offsets]
    fourth = swap_ranks(blocks, 3)
    second = swap_ranks(blocks, 2)
    third = swap_ranks(blocks, 1)
    u_high, u_t_high, d, d_t, _, got_order = fetch(
        place,
        (w_up, w_down),
        (Piece(0, 0, piece, half - piece, 3), Piece(1, 1, 0, half, 4)),
        blocks,
        (16, 128),
        lambda place: gathered_order(plan, place[2]),
        BATCH * plan.rows,
    )

    (mine,) = on_core(
        functools.partial(up_kernel, plan, ranks),
        None,
        (got_order, blocks, second, third, fourth, g, u_low, u_high, d_t),
        [((2 * ranks, (groups + len(plan.places)) * hid), F32)],
        3 * hid * half,
    )
    kept, sent = on_core(
        functools.partial(down_kernel, plan, ranks),
        place,
        (back_order, mine, swap_cores(mine), g_t, u_t_low, u_t_high, d),
        [((ranks // 2 * PARTS * groups * 2, half // PARTS), BF16)] * 2,
        3 * hid * half,
    )
    weights = jnp.concatenate(
        [
            expert_weights(after(fwd_routes[0], sent), fwd_probs[0]),
            expert_weights(after(bwd_routes[0], sent), bwd_probs[0]),
        ]
    )
    even, odd = by_section(weights, swap_cores(weights), core)
    far = to_next_chips(odd[:2], even[2:], 0)
    weights = jnp.concatenate([even[:2], far[0], odd[2:], *far[1:]])
    weights = jnp.concatenate([weights] * PARTS)
    block = ((PARTS * groups * 2, half // PARTS), BF16)
    pairs = on_core(
        pair_kernel, None, (kept, swap_ranks(sent, 1), weights), [block] * (ranks // 2), half
    )
    pairs = dict(zip(offsets, pairs, strict=True))
    offsets = [0] + sorted(offsets[1:], reverse=True)
    back = [swap_ranks(pairs[o], o) if o else pairs[o] for o in offsets]
    columns, chosen = on_core(
        functools.partial(select_kernel, plan, offsets, shards),
        place,
        (weights,),
        [((len(offsets) * weights.shape[0], 128), F32), ((8 * PARTS, weights.shape[0]), BF16)],
        half,
    )
    own, other = on_core(
        finish_kernel,
        None,
        (columns, chosen, *back),
        [((4 * PARTS, half // PARTS), BF16)] * 2,
        half,
    )
    own, other = unfolded(own), unfolded(swap_cores(other))
    whole = jnp.where(
        core == 0,
        jnp.concatenate([own, other], axis=1),
        jnp.concatenate([other, own], axis=1),
    )
    return (whole[None, :2], whole[None, 2:])


def solution(mesh):
    return jax.shard_map(
        local,
        mesh=mesh,
        in_specs=(
            P("section", "expert", None),
            P("section", "expert", None),
            P("section", "expert", None),
            P("section", "expert", None),
            P("section", "expert", None),
            P("section", "expert", None),
            P("section", "expert", None),
            P(None, "expert"),
            P(None, "expert"),
            P("expert", None),
        ),
        out_specs=(P("section", "expert", None), P("section", "expert", None)),
        check_vma=False,
    )
```

```python
import functools
import typing

import jax
import jax.numpy as jnp
from jax import lax
from jax.experimental import pallas as pl
from jax.experimental.pallas import tpu as pltpu
from jax.sharding import PartitionSpec as P

GROUPS = 4
PARTS = 4
BATCH = 8
F32 = jnp.float32
BF16 = jnp.bfloat16


def swap_cores(block):
    sections = range(lax.axis_size("section"))
    return lax.ppermute(block, "section", [(i, i ^ 1) for i in sections])


def expert_weights(routes, probs):
    named = routes[:, :, None] == jnp.arange(GROUPS, dtype=jnp.int32)
    return jnp.sum(jnp.where(named, probs[:, :, None], 0.0), axis=1)


def by_section(mine, theirs, core):
    return jnp.where(core == 0, mine, theirs), jnp.where(core == 0, theirs, mine)


def swap_ranks(block, bit):
    ranks = range(lax.axis_size("expert"))
    return lax.ppermute(block, "expert", [(i, i ^ bit) for i in ranks])


def to_next_chips(fwd, bwd, bit):
    sections, ranks = lax.axis_size("section"), lax.axis_size("expert")

    def move(block, pairs):
        route = [(a * ranks + e, b * ranks + (e ^ bit)) for a, b in pairs for e in range(ranks)]
        return lax.ppermute(block, ("section", "expert"), route)

    up = [(i, i + 2) for i in range(sections - 2)]
    down = [(b, a) for a, b in up]
    if sections != 4:
        return [move(fwd, up), move(bwd, down)]
    return [move(jnp.where(lax.axis_index("section") < 2, fwd, bwd), up + down)]


def folded(block):
    rows, width = block.shape
    block = block.reshape(rows, PARTS, width // PARTS).transpose(1, 0, 2)
    return block.reshape(rows * PARTS, width // PARTS)


def unfolded(block):
    rows, width = block.shape
    block = block.reshape(PARTS, rows // PARTS, width).transpose(1, 0, 2)
    return block.reshape(rows // PARTS, width * PARTS)


class Plan(typing.NamedTuple):
    fwd: int
    both: int
    bwd: int
    rows: int
    places: tuple
    other: tuple


def plan_of(sections):
    if sections == 4:
        places = ((0, 2, 0), (24, 4, 0), (8, 4, 0), (24, 4, 2), (8, 4, 2))
        other = (None, (24, 2, 0), None, (32, 2, 0), None)
        return Plan(1, 1, 1, 40, places, other)
    places = ((0, 2, 0), (24, 2, 0), (8, 4, 0), (32, 4, 0), (8, 4, 2), (32, 4, 2))
    return Plan(2, 0, 2, 48, places, (None,) * 6)


def dot(a, b):
    return jnp.dot(a, b, preferred_element_type=F32)


def one_hot(rows, want):
    out = lax.broadcasted_iota(jnp.int32, (rows, rows), 0)
    src = lax.broadcasted_iota(jnp.int32, (rows, rows), 1)
    return jnp.where(want(out) == src, 1.0, 0.0).astype(BF16)


def gathered_order(plan, forward):
    kinds = len(plan.places)

    def want(out):
        part, rest = lax.div(out, kinds * 2 * BATCH), lax.rem(out, kinds * 2 * BATCH)
        kind, rest = lax.div(rest, 2 * BATCH), lax.rem(rest, 2 * BATCH)
        row = jnp.zeros_like(out)
        for i, (here, there) in enumerate(zip(plan.places, plan.other, strict=True)):
            base, size, offset = here
            if there is not None:
                base, size, offset = (
                    jnp.where(forward == 1, t, h) for h, t in zip(here, there, strict=True)
                )
            row = jnp.where(kind == i, base + offset + part * size, row)
        return lax.div(rest, 2) * plan.rows + row + lax.rem(rest, 2)

    return one_hot(BATCH * plan.rows, want)


def returned_order(groups):
    size = PARTS * groups * 2

    def want(out):
        block, rest = lax.div(out, size), lax.rem(out, size)
        return lax.div(rest, 2) * (2 * BATCH) + block * 2 + lax.rem(rest, 2)

    return one_hot(BATCH * size, want)


class Piece(typing.NamedTuple):
    weight: int
    axis: int
    start: int
    size: int
    steps: int


def fetch_kernel(pieces, order, place, *refs):
    count = 1 + max(piece.weight for piece in pieces)
    weights, refs = refs[:count], refs[count + 1 :]
    *outs, zero, made, sems = refs
    copies = []
    for i, piece in enumerate(pieces):
        weight, held = weights[piece.weight], outs[2 * i]
        half = weight.shape[piece.axis] // 2
        size = piece.size // piece.steps
        for step in range(piece.steps):
            start = place[0] * half + piece.start + step * size
            there = pl.ds(pl.multiple_of(start, 128), size)
            here = pl.ds(step * size, size)
            if piece.axis == 1:
                there, here = (slice(None), there), (slice(None), here)
            sem = sems.at[len(copies)]
            copies.append(pltpu.make_async_copy(weight.at[there], held.at[here], sem))
    for copy in copies:
        copy.start()
    zero[...] = jnp.zeros_like(zero)
    made[...] = order(place)
    copies = iter(copies)
    for i, piece in enumerate(pieces):
        held, turned = outs[2 * i : 2 * i + 2]
        size = piece.size // piece.steps
        for step in range(piece.steps):
            next(copies).wait()
            here = slice(step * size, (step + 1) * size)
            if piece.axis == 0:
                turned[:, here] = held[here, :].T
            else:
                turned[here, :] = held[:, here].T


def fetch(place, weights, pieces, earlier, like, order, count):
    shapes = []
    for piece in pieces:
        shape = list(weights[piece.weight].shape)
        shape[piece.axis] = piece.size
        shapes += [tuple(shape), tuple(shape[::-1])]
    nbytes = sum(piece.size for piece in pieces) * weights[0].shape[1] * 4
    steps = sum(piece.steps for piece in pieces)
    return pl.pallas_call(
        functools.partial(fetch_kernel, pieces, order),
        in_specs=[pl.BlockSpec(memory_space=pltpu.SMEM)]
        + [pl.BlockSpec(memory_space=pltpu.HBM)] * len(weights)
        + [pl.BlockSpec(memory_space=pl.ANY)],
        out_specs=[pl.BlockSpec(memory_space=pltpu.VMEM)] * (len(shapes) + 2),
        out_shape=[pltpu.VMEM(shape, BF16) for shape in shapes]
        + [jax.ShapeDtypeStruct(like, BF16), pltpu.VMEM((count, count), BF16)],
        scratch_shapes=[pltpu.SemaphoreType.DMA((steps,))],
        compiler_params=pltpu.CompilerParams(vmem_limit_bytes=2**21),
        cost_estimate=pl.CostEstimate(flops=0, bytes_accessed=nbytes, transcendentals=0),
    )(
        place,
        *[pltpu.with_memory_space_constraint(weight, pltpu.HBM) for weight in weights],
        earlier,
    )


def up_kernel(plan, ranks, order, first, second, third, fourth, g, u_low, u_high, d_t, out):
    hid = g.shape[1]
    n = 2 * BATCH
    kinds = len(plan.places)
    groups = plan.fwd + plan.both + plan.bwd
    piece = first.shape[1]
    blocks = jnp.concatenate([first[...], second[...], third[...], fourth[...]])
    order = order[...]
    count = order.shape[0]
    batches = ranks // BATCH
    sorted_rows = [
        dot(order, blocks[i * count : (i + 1) * count]).astype(BF16) for i in range(batches)
    ]
    a, b, dh = 0.0, 0.0, 0.0
    for part in range(PARTS):
        cols = slice(part * piece, (part + 1) * piece)
        at = [(part * kinds + kind) * n for kind in range(kinds)]
        taken = [jnp.concatenate([rows[i : i + n] for rows in sorted_rows]) for i in at]
        rows = jnp.concatenate(taken[:groups])
        a += dot(rows, g[cols, :])
        u = u_high[(part - 1) * piece : part * piece, :] if part else u_low[...]
        b += dot(rows, u)
        dh += dot(jnp.concatenate(taken[groups:]), d_t[cols, :])
    n = n * batches
    for i in range(groups):
        out[:, i * hid : (i + 1) * hid] = a[i * n : (i + 1) * n]
        out[:, (groups + i) * hid : (groups + i + 1) * hid] = b[i * n : (i + 1) * n]
    for i in range(kinds - groups):
        at = (2 * groups + i) * hid
        out[:, at : at + hid] = dh[i * n : (i + 1) * n]


def down_kernel(plan, ranks, place, _, order, mine, theirs, g_t, u_t_low, u_t_high, d, kept, sent):
    hid = d.shape[0]
    groups = plan.fwd + plan.both + plan.bwd
    n = 2 * ranks
    split = plan.fwd * n

    def summed(i):
        return mine[:, i * hid : (i + 1) * hid] + theirs[:, i * hid : (i + 1) * hid]

    h, da, du = [], [], []
    forward = jnp.where(place[2] == 1, 1.0, 0.0)
    for i in range(groups):
        a, b = summed(i), summed(groups + i)
        s = jax.nn.sigmoid(a)
        if i < plan.fwd + plan.both:
            hidden = (a * s * b).astype(BF16)
            h.append(hidden if i < plan.fwd else hidden * forward.astype(BF16))
        if i >= plan.fwd:
            dh = summed(2 * groups + i - plan.fwd)
            da.append((dh * b * s * (1.0 + a * (1.0 - s))).astype(BF16))
            du.append((dh * a * s).astype(BF16))
    h, da, du = jnp.concatenate(h), jnp.concatenate(da), jnp.concatenate(du)
    piece = kept.shape[1]
    results = []
    for part in range(PARTS):
        cols = slice(part * piece, (part + 1) * piece)
        y = dot(h, d[:, cols])
        u_t = u_t_high[:, (part - 1) * piece : part * piece] if part else u_t_low[...]
        dx = dot(da, g_t[:, cols]) + dot(du, u_t)
        shared = plan.both * n
        rows = [y[:split], y[split:] + dx[:shared], dx[shared:]] if shared else [y, dx]
        results.append(jnp.concatenate(rows).astype(BF16))
    order = order[...]
    size = 2 * BATCH
    rows = [
        jnp.concatenate(
            [
                result[i * n + batch * size : i * n + (batch + 1) * size]
                for result in results
                for i in range(groups)
            ]
        )
        for batch in range(ranks // BATCH)
    ]
    rows = jnp.concatenate([dot(order, batch).astype(BF16) for batch in rows])
    kept[...] = rows[: kept.shape[0]]
    sent[...] = rows[kept.shape[0] :]


def pair_kernel(kept, got, weights, *pairs):
    size = pairs[0].shape[0]
    for i, pair in enumerate(pairs):
        rows = slice(i * size, (i + 1) * size)
        pair[...] = (kept[rows].astype(F32) + got[rows].astype(F32)).astype(BF16)


def select_kernel(plan, offsets, shards, place, weights, columns, chosen):
    size = weights.shape[0]
    for i, offset in enumerate(offsets):
        expert = lax.div(lax.bitwise_xor(place[1], jnp.int32(offset)), jnp.int32(shards))
        named = lax.broadcasted_iota(jnp.int32, weights.shape, 1) == expert
        weight = jnp.sum(jnp.where(named, weights[...], 0.0), axis=1, keepdims=True)
        columns[i * size : (i + 1) * size, :] = jnp.broadcast_to(weight, (size, 128))
    out = lax.broadcasted_iota(jnp.int32, chosen.shape, 0)
    src = lax.broadcasted_iota(jnp.int32, chosen.shape, 1)
    odd = jnp.where(out < 4 * PARTS, place[0], 1 - place[0])
    part, row = lax.rem(lax.div(out, 4), PARTS), lax.rem(out, 4)
    bwd = lax.div(row, 2)
    if plan.both:
        far = jnp.where(place[2] == 1, 0, 1)
        group = jnp.where(bwd == odd, 1, 2 * bwd)
        present = (bwd != odd) | (bwd == far)
    else:
        group = 2 * bwd + jnp.where(bwd == odd, 1, 0)
        present = out >= 0
    groups = plan.fwd + plan.both + plan.bwd
    want = part * (2 * groups) + group * 2 + lax.rem(row, 2)
    chosen[...] = jnp.where((want == src) & present, 1.0, 0.0).astype(BF16)


def finish_kernel(columns, chosen, *refs):
    *back, own, other = refs
    size = back[0].shape[0]
    total = 0.0
    for i, block in enumerate(back):
        total += block[...].astype(F32) * columns[i * size : (i + 1) * size, :1]
    rows = dot(chosen[...], total.astype(BF16)).astype(BF16)
    own[...] = rows[: own.shape[0]]
    other[...] = rows[own.shape[0] :]


def on_core(kernel, place, operands, results, cost):
    specs = [pl.BlockSpec(memory_space=pltpu.VMEM)] * len(operands)
    operands = [pltpu.with_memory_space_constraint(x, pltpu.VMEM) for x in operands]
    if place is not None:
        specs = [pl.BlockSpec(memory_space=pltpu.SMEM)] + specs
        operands = [place] + operands
    ranks = lax.axis_size("expert")
    return pl.pallas_call(
        kernel,
        in_specs=specs,
        out_specs=[pl.BlockSpec(memory_space=pltpu.VMEM)] * len(results),
        out_shape=[jax.ShapeDtypeStruct(*result) for result in results],
        compiler_params=pltpu.CompilerParams(vmem_limit_bytes=ranks * 3 * 2**17),
        cost_estimate=pl.CostEstimate(
            flops=cost * 512, bytes_accessed=cost * 2, transcendentals=0
        ),
    )(*operands)


def after(value, other):
    return lax.optimization_barrier((value, other))[0]


def local(
    fwd_tokens,
    fwd_routes,
    fwd_probs,
    bwd_tokens,
    bwd_routes,
    bwd_probs,
    bwd_grads,
    w_gate,
    w_up,
    w_down,
):
    ranks, sections = lax.axis_size("expert"), lax.axis_size("section")
    shards = ranks // GROUPS
    plan = plan_of(sections)
    groups = plan.fwd + plan.both + plan.bwd
    width = fwd_tokens.shape[2]
    half = width // 2
    hid = w_gate.shape[1]
    section = lax.axis_index("section")
    core = section % 2
    place = jnp.stack([core, lax.axis_index("expert"), section >= 2]).astype(jnp.int32)

    inputs = [fwd_tokens[0], bwd_tokens[0], bwd_grads[0]]
    theirs = jnp.concatenate([swap_cores(block) for block in inputs])
    mine = jnp.concatenate(inputs)
    mine, theirs = (
        jnp.where(core == 0, rows[:, :half], rows[:, half:]) for rows in (mine, theirs)
    )
    even, odd = by_section(mine, theirs, core)

    near = jnp.concatenate([folded(even[:2]), folded(odd[2:])])
    far_fwd, far_bwd = folded(odd[:2]), folded(even[2:])
    if plan.both:
        far_fwd = jnp.pad(far_fwd, ((0, far_bwd.shape[0] - far_fwd.shape[0]), (0, 0)))
    top = ranks // 2
    far = to_next_chips(far_fwd, far_bwd, 0)
    far_top = to_next_chips(far_fwd, far_bwd, top)
    blocks = jnp.concatenate([near, *far, swap_ranks(near, top), *far_top])
    offsets = [0, top]
    piece = half // PARTS
    g, g_t, u_low, u_t_low, zero, back_order = fetch(
        place,
        (w_gate, w_up),
        (Piece(0, 0, 0, half, 4), Piece(1, 0, 0, piece, 1)),
        near,
        blocks.shape,
        lambda _: returned_order(groups),
        BATCH * PARTS * groups * 2,
    )
    blocks = blocks + zero
    bit = top // 2
    while bit > 2:
        blocks = jnp.concatenate([blocks, swap_ranks(blocks, bit)])
        offsets += [o ^ bit for o in offsets]
        bit //= 2
    offsets += [o ^ 2 for o in offsets]
    fourth = swap_ranks(blocks, 3)
    second = swap_ranks(blocks, 2)
    third = swap_ranks(blocks, 1)
    u_high, u_t_high, d, d_t, _, got_order = fetch(
        place,
        (w_up, w_down),
        (Piece(0, 0, piece, half - piece, 3), Piece(1, 1, 0, half, 4)),
        blocks,
        (16, 128),
        lambda place: gathered_order(plan, place[2]),
        BATCH * plan.rows,
    )

    (mine,) = on_core(
        functools.partial(up_kernel, plan, ranks),
        None,
        (got_order, blocks, second, third, fourth, g, u_low, u_high, d_t),
        [((2 * ranks, (groups + len(plan.places)) * hid), F32)],
        3 * hid * half,
    )
    weights = jnp.concatenate(
        [
            expert_weights(after(fwd_routes[0], mine), fwd_probs[0]),
            expert_weights(after(bwd_routes[0], mine), bwd_probs[0]),
        ]
    )
    others = swap_cores(weights)
    even, odd = by_section(weights, others, core)
    kept, sent = on_core(
        functools.partial(down_kernel, plan, ranks),
        place,
        (others, back_order, mine, swap_cores(mine), g_t, u_t_low, u_t_high, d),
        [((ranks // 2 * PARTS * groups * 2, half // PARTS), BF16)] * 2,
        3 * hid * half,
    )
    far = to_next_chips(odd[:2], even[2:], 0)
    weights = jnp.concatenate([even[:2], far[0], odd[2:], *far[1:]])
    weights = jnp.concatenate([weights] * PARTS)
    block = ((PARTS * groups * 2, half // PARTS), BF16)
    pairs = on_core(
        pair_kernel, None, (kept, swap_ranks(sent, 1), weights), [block] * (ranks // 2), half
    )
    pairs = dict(zip(offsets, pairs, strict=True))
    offsets = [0] + sorted(offsets[1:], reverse=True)
    back = [swap_ranks(pairs[o], o) if o else pairs[o] for o in offsets]
    columns, chosen = on_core(
        functools.partial(select_kernel, plan, offsets, shards),
        place,
        (weights,),
        [((len(offsets) * weights.shape[0], 128), F32), ((8 * PARTS, weights.shape[0]), BF16)],
        half,
    )
    own, other = on_core(
        finish_kernel,
        None,
        (columns, chosen, *back),
        [((4 * PARTS, half // PARTS), BF16)] * 2,
        half,
    )
    own, other = unfolded(own), unfolded(swap_cores(other))
    whole = jnp.where(
        core == 0,
        jnp.concatenate([own, other], axis=1),
        jnp.concatenate([other, own], axis=1),
    )
    return (whole[None, :2], whole[None, 2:])


def solution(mesh):
    return jax.shard_map(
        local,
        mesh=mesh,
        in_specs=(
            P("section", "expert", None),
            P("section", "expert", None),
            P("section", "expert", None),
            P("section", "expert", None),
            P("section", "expert", None),
            P("section", "expert", None),
            P("section", "expert", None),
            P(None, "expert"),
            P(None, "expert"),
            P("expert", None),
        ),
        out_specs=(P("section", "expert", None), P("section", "expert", None)),
        check_vma=False,
    )
```

```python
import functools
import typing

import jax
import jax.numpy as jnp
from jax import lax
from jax.experimental import pallas as pl
from jax.experimental.pallas import tpu as pltpu
from jax.sharding import PartitionSpec as P

GROUPS = 4
PARTS = 4
BATCH = 8
F32 = jnp.float32
BF16 = jnp.bfloat16


def swap_cores(block):
    sections = range(lax.axis_size("section"))
    return lax.ppermute(block, "section", [(i, i ^ 1) for i in sections])


def expert_weights(routes, probs):
    named = routes[:, :, None] == jnp.arange(GROUPS, dtype=jnp.int32)
    return jnp.sum(jnp.where(named, probs[:, :, None], 0.0), axis=1)


def by_section(mine, theirs, core):
    return jnp.where(core == 0, mine, theirs), jnp.where(core == 0, theirs, mine)


def swap_ranks(block, bit):
    ranks = range(lax.axis_size("expert"))
    return lax.ppermute(block, "expert", [(i, i ^ bit) for i in ranks])


def to_next_chips(fwd, bwd, bit):
    sections, ranks = lax.axis_size("section"), lax.axis_size("expert")

    def move(block, pairs):
        route = [(a * ranks + e, b * ranks + (e ^ bit)) for a, b in pairs for e in range(ranks)]
        return lax.ppermute(block, ("section", "expert"), route)

    up = [(i, i + 2) for i in range(sections - 2)]
    down = [(b, a) for a, b in up]
    if sections != 4:
        return [move(fwd, up), move(bwd, down)]
    return [move(jnp.where(lax.axis_index("section") < 2, fwd, bwd), up + down)]


def folded(block):
    rows, width = block.shape
    block = block.reshape(rows, PARTS, width // PARTS).transpose(1, 0, 2)
    return block.reshape(rows * PARTS, width // PARTS)


def unfolded(block):
    rows, width = block.shape
    block = block.reshape(PARTS, rows // PARTS, width).transpose(1, 0, 2)
    return block.reshape(rows // PARTS, width * PARTS)


class Plan(typing.NamedTuple):
    fwd: int
    both: int
    bwd: int
    rows: int
    places: tuple
    other: tuple


def plan_of(sections):
    if sections == 4:
        places = ((0, 2, 0), (24, 4, 0), (8, 4, 0), (24, 4, 2), (8, 4, 2))
        other = (None, (24, 2, 0), None, (32, 2, 0), None)
        return Plan(1, 1, 1, 40, places, other)
    places = ((0, 2, 0), (24, 2, 0), (8, 4, 0), (32, 4, 0), (8, 4, 2), (32, 4, 2))
    return Plan(2, 0, 2, 48, places, (None,) * 6)


def dot(a, b):
    return jnp.dot(a, b, preferred_element_type=F32)


def one_hot(rows, want):
    out = lax.broadcasted_iota(jnp.int32, (rows, rows), 0)
    src = lax.broadcasted_iota(jnp.int32, (rows, rows), 1)
    return jnp.where(want(out) == src, 1.0, 0.0).astype(BF16)


def gathered_order(plan, forward):
    kinds = len(plan.places)

    def want(out):
        part, rest = lax.div(out, kinds * 2 * BATCH), lax.rem(out, kinds * 2 * BATCH)
        kind, rest = lax.div(rest, 2 * BATCH), lax.rem(rest, 2 * BATCH)
        row = jnp.zeros_like(out)
        for i, (here, there) in enumerate(zip(plan.places, plan.other, strict=True)):
            base, size, offset = here
            if there is not None:
                base, size, offset = (
                    jnp.where(forward == 1, t, h) for h, t in zip(here, there, strict=True)
                )
            row = jnp.where(kind == i, base + offset + part * size, row)
        return lax.div(rest, 2) * plan.rows + row + lax.rem(rest, 2)

    return one_hot(BATCH * plan.rows, want)


def returned_order(groups):
    size = PARTS * groups * 2

    def want(out):
        block, rest = lax.div(out, size), lax.rem(out, size)
        return lax.div(rest, 2) * (2 * BATCH) + block * 2 + lax.rem(rest, 2)

    return one_hot(BATCH * size, want)


class Piece(typing.NamedTuple):
    weight: int
    axis: int
    start: int
    size: int
    steps: int


def fetch_kernel(pieces, order, place, *refs):
    count = 1 + max(piece.weight for piece in pieces)
    weights, refs = refs[:count], refs[count + 1 :]
    *outs, zero, made, sems = refs
    copies = []
    for i, piece in enumerate(pieces):
        weight, held = weights[piece.weight], outs[2 * i]
        half = weight.shape[piece.axis] // 2
        size = piece.size // piece.steps
        for step in range(piece.steps):
            start = place[0] * half + piece.start + step * size
            there = pl.ds(pl.multiple_of(start, 128), size)
            here = pl.ds(step * size, size)
            if piece.axis == 1:
                there, here = (slice(None), there), (slice(None), here)
            sem = sems.at[len(copies)]
            copies.append(pltpu.make_async_copy(weight.at[there], held.at[here], sem))
    for copy in copies:
        copy.start()
    zero[...] = jnp.zeros_like(zero)
    made[...] = order(place)
    copies = iter(copies)
    for i, piece in enumerate(pieces):
        held, turned = outs[2 * i : 2 * i + 2]
        size = piece.size // piece.steps
        for step in range(piece.steps):
            next(copies).wait()
            here = slice(step * size, (step + 1) * size)
            if piece.axis == 0:
                turned[:, here] = held[here, :].T
            else:
                turned[here, :] = held[:, here].T


def fetch(place, weights, pieces, earlier, like, order, count):
    shapes = []
    for piece in pieces:
        shape = list(weights[piece.weight].shape)
        shape[piece.axis] = piece.size
        shapes += [tuple(shape), tuple(shape[::-1])]
    nbytes = sum(piece.size for piece in pieces) * weights[0].shape[1] * 4
    steps = sum(piece.steps for piece in pieces)
    return pl.pallas_call(
        functools.partial(fetch_kernel, pieces, order),
        in_specs=[pl.BlockSpec(memory_space=pltpu.SMEM)]
        + [pl.BlockSpec(memory_space=pltpu.HBM)] * len(weights)
        + [pl.BlockSpec(memory_space=pl.ANY)],
        out_specs=[pl.BlockSpec(memory_space=pltpu.VMEM)] * (len(shapes) + 2),
        out_shape=[pltpu.VMEM(shape, BF16) for shape in shapes]
        + [jax.ShapeDtypeStruct(like, BF16), pltpu.VMEM((count, count), BF16)],
        scratch_shapes=[pltpu.SemaphoreType.DMA((steps,))],
        compiler_params=pltpu.CompilerParams(vmem_limit_bytes=2**21),
        cost_estimate=pl.CostEstimate(flops=0, bytes_accessed=nbytes, transcendentals=0),
    )(
        place,
        *[pltpu.with_memory_space_constraint(weight, pltpu.HBM) for weight in weights],
        earlier,
    )


def up_kernel(plan, ranks, order, first, second, third, fourth, g, u_low, u_high, d_t, out):
    hid = g.shape[1]
    n = 2 * BATCH
    kinds = len(plan.places)
    groups = plan.fwd + plan.both + plan.bwd
    piece = first.shape[1]
    blocks = jnp.concatenate([first[...], second[...], third[...], fourth[...]])
    order = order[...]
    count = order.shape[0]
    batches = ranks // BATCH
    sorted_rows = [
        dot(order, blocks[i * count : (i + 1) * count]).astype(BF16) for i in range(batches)
    ]
    a, b, dh = 0.0, 0.0, 0.0
    for part in range(PARTS):
        cols = slice(part * piece, (part + 1) * piece)
        at = [(part * kinds + kind) * n for kind in range(kinds)]
        taken = [jnp.concatenate([rows[i : i + n] for rows in sorted_rows]) for i in at]
        rows = jnp.concatenate(taken[:groups])
        a += dot(rows, g[cols, :])
        u = u_high[(part - 1) * piece : part * piece, :] if part else u_low[...]
        b += dot(rows, u)
        dh += dot(jnp.concatenate(taken[groups:]), d_t[cols, :])
    n = n * batches
    for i in range(groups):
        out[:, i * hid : (i + 1) * hid] = a[i * n : (i + 1) * n]
        out[:, (groups + i) * hid : (groups + i + 1) * hid] = b[i * n : (i + 1) * n]
    for i in range(kinds - groups):
        at = (2 * groups + i) * hid
        out[:, at : at + hid] = dh[i * n : (i + 1) * n]


def down_kernel(plan, ranks, place, _, order, mine, theirs, g_t, u_t_low, u_t_high, d, kept, sent):
    hid = d.shape[0]
    groups = plan.fwd + plan.both + plan.bwd
    n = 2 * ranks
    split = plan.fwd * n

    def summed(i):
        return mine[:, i * hid : (i + 1) * hid] + theirs[:, i * hid : (i + 1) * hid]

    h, da, du = [], [], []
    forward = jnp.where(place[2] == 1, 1.0, 0.0)
    for i in range(groups):
        a, b = summed(i), summed(groups + i)
        s = jax.nn.sigmoid(a)
        if i < plan.fwd + plan.both:
            hidden = (a * s * b).astype(BF16)
            h.append(hidden if i < plan.fwd else hidden * forward.astype(BF16))
        if i >= plan.fwd:
            dh = summed(2 * groups + i - plan.fwd)
            da.append((dh * b * s * (1.0 + a * (1.0 - s))).astype(BF16))
            du.append((dh * a * s).astype(BF16))
    h, da, du = jnp.concatenate(h), jnp.concatenate(da), jnp.concatenate(du)
    piece = kept.shape[1]
    results = []
    for part in range(PARTS):
        cols = slice(part * piece, (part + 1) * piece)
        y = dot(h, d[:, cols])
        u_t = u_t_high[:, (part - 1) * piece : part * piece] if part else u_t_low[...]
        dx = dot(da, g_t[:, cols]) + dot(du, u_t)
        shared = plan.both * n
        rows = [y[:split], y[split:] + dx[:shared], dx[shared:]] if shared else [y, dx]
        results.append(jnp.concatenate(rows).astype(BF16))
    order = order[...]
    size = 2 * BATCH
    rows = [
        jnp.concatenate(
            [
                result[i * n + batch * size : i * n + (batch + 1) * size]
                for result in results
                for i in range(groups)
            ]
        )
        for batch in range(ranks // BATCH)
    ]
    rows = jnp.concatenate([dot(order, batch).astype(BF16) for batch in rows])
    kept[...] = rows[: kept.shape[0]]
    sent[...] = rows[kept.shape[0] :]


def pair_kernel(kept, got, weights, *pairs):
    size = pairs[0].shape[0]
    total = kept[...].astype(F32) + got[...].astype(F32)
    for i, pair in enumerate(pairs):
        pair[...] = total[i * size : (i + 1) * size].astype(BF16)


def select_kernel(plan, offsets, shards, place, weights, columns, chosen):
    size = weights.shape[0]
    for i, offset in enumerate(offsets):
        expert = lax.div(lax.bitwise_xor(place[1], jnp.int32(offset)), jnp.int32(shards))
        named = lax.broadcasted_iota(jnp.int32, weights.shape, 1) == expert
        weight = jnp.sum(jnp.where(named, weights[...], 0.0), axis=1, keepdims=True)
        columns[i * size : (i + 1) * size, :] = jnp.broadcast_to(weight, (size, 128))
    out = lax.broadcasted_iota(jnp.int32, chosen.shape, 0)
    src = lax.broadcasted_iota(jnp.int32, chosen.shape, 1)
    odd = jnp.where(out < 4 * PARTS, place[0], 1 - place[0])
    part, row = lax.rem(lax.div(out, 4), PARTS), lax.rem(out, 4)
    bwd = lax.div(row, 2)
    if plan.both:
        far = jnp.where(place[2] == 1, 0, 1)
        group = jnp.where(bwd == odd, 1, 2 * bwd)
        present = (bwd != odd) | (bwd == far)
    else:
        group = 2 * bwd + jnp.where(bwd == odd, 1, 0)
        present = out >= 0
    groups = plan.fwd + plan.both + plan.bwd
    want = part * (2 * groups) + group * 2 + lax.rem(row, 2)
    chosen[...] = jnp.where((want == src) & present, 1.0, 0.0).astype(BF16)


def finish_kernel(columns, chosen, *refs):
    *back, own, other = refs
    size = back[0].shape[0]
    total = 0.0
    for i, block in enumerate(back):
        total += block[...].astype(F32) * columns[i * size : (i + 1) * size, :1]
    rows = dot(chosen[...], total.astype(BF16)).astype(BF16)
    own[...] = rows[: own.shape[0]]
    other[...] = rows[own.shape[0] :]


def on_core(kernel, place, operands, results, cost):
    specs = [pl.BlockSpec(memory_space=pltpu.VMEM)] * len(operands)
    operands = [pltpu.with_memory_space_constraint(x, pltpu.VMEM) for x in operands]
    if place is not None:
        specs = [pl.BlockSpec(memory_space=pltpu.SMEM)] + specs
        operands = [place] + operands
    ranks = lax.axis_size("expert")
    return pl.pallas_call(
        kernel,
        in_specs=specs,
        out_specs=[pl.BlockSpec(memory_space=pltpu.VMEM)] * len(results),
        out_shape=[jax.ShapeDtypeStruct(*result) for result in results],
        compiler_params=pltpu.CompilerParams(vmem_limit_bytes=ranks * 3 * 2**17),
        cost_estimate=pl.CostEstimate(
            flops=cost * 512, bytes_accessed=cost * 2, transcendentals=0
        ),
    )(*operands)


def after(value, other):
    return lax.optimization_barrier((value, other))[0]


def local(
    fwd_tokens,
    fwd_routes,
    fwd_probs,
    bwd_tokens,
    bwd_routes,
    bwd_probs,
    bwd_grads,
    w_gate,
    w_up,
    w_down,
):
    ranks, sections = lax.axis_size("expert"), lax.axis_size("section")
    shards = ranks // GROUPS
    plan = plan_of(sections)
    groups = plan.fwd + plan.both + plan.bwd
    width = fwd_tokens.shape[2]
    half = width // 2
    hid = w_gate.shape[1]
    section = lax.axis_index("section")
    core = section % 2
    place = jnp.stack([core, lax.axis_index("expert"), section >= 2]).astype(jnp.int32)

    inputs = [fwd_tokens[0], bwd_tokens[0], bwd_grads[0]]
    theirs = jnp.concatenate([swap_cores(block) for block in inputs])
    mine = jnp.concatenate(inputs)
    mine, theirs = (
        jnp.where(core == 0, rows[:, :half], rows[:, half:]) for rows in (mine, theirs)
    )
    even, odd = by_section(mine, theirs, core)

    near = jnp.concatenate([folded(even[:2]), folded(odd[2:])])
    far_fwd, far_bwd = folded(odd[:2]), folded(even[2:])
    if plan.both:
        far_fwd = jnp.pad(far_fwd, ((0, far_bwd.shape[0] - far_fwd.shape[0]), (0, 0)))
    top = ranks // 2
    far = to_next_chips(far_fwd, far_bwd, 0)
    far_top = to_next_chips(far_fwd, far_bwd, top)
    blocks = jnp.concatenate([near, *far, swap_ranks(near, top), *far_top])
    offsets = [0, top]
    piece = half // PARTS
    g, g_t, u_low, u_t_low, zero, back_order = fetch(
        place,
        (w_gate, w_up),
        (Piece(0, 0, 0, half, 4), Piece(1, 0, 0, piece, 1)),
        near,
        blocks.shape,
        lambda _: returned_order(groups),
        BATCH * PARTS * groups * 2,
    )
    blocks = blocks + zero
    bit = top // 2
    while bit > 2:
        blocks = jnp.concatenate([blocks, swap_ranks(blocks, bit)])
        offsets += [o ^ bit for o in offsets]
        bit //= 2
    offsets += [o ^ 2 for o in offsets]
    fourth = swap_ranks(blocks, 3)
    second = swap_ranks(blocks, 2)
    third = swap_ranks(blocks, 1)
    u_high, u_t_high, d, d_t, _, got_order = fetch(
        place,
        (w_up, w_down),
        (Piece(0, 0, piece, half - piece, 3), Piece(1, 1, 0, half, 4)),
        blocks,
        (16, 128),
        lambda place: gathered_order(plan, place[2]),
        BATCH * plan.rows,
    )

    (mine,) = on_core(
        functools.partial(up_kernel, plan, ranks),
        None,
        (got_order, blocks, second, third, fourth, g, u_low, u_high, d_t),
        [((2 * ranks, (groups + len(plan.places)) * hid), F32)],
        3 * hid * half,
    )
    weights = jnp.concatenate(
        [
            expert_weights(after(fwd_routes[0], mine), fwd_probs[0]),
            expert_weights(after(bwd_routes[0], mine), bwd_probs[0]),
        ]
    )
    others = swap_cores(weights)
    even, odd = by_section(weights, others, core)
    kept, sent = on_core(
        functools.partial(down_kernel, plan, ranks),
        place,
        (others, back_order, mine, swap_cores(mine), g_t, u_t_low, u_t_high, d),
        [((ranks // 2 * PARTS * groups * 2, half // PARTS), BF16)] * 2,
        3 * hid * half,
    )
    far = to_next_chips(odd[:2], even[2:], 0)
    weights = jnp.concatenate([even[:2], far[0], odd[2:], *far[1:]])
    weights = jnp.concatenate([weights] * PARTS)
    block = ((PARTS * groups * 2, half // PARTS), BF16)
    pairs = on_core(
        pair_kernel, None, (kept, swap_ranks(sent, 1), weights), [block] * (ranks // 2), half
    )
    pairs = dict(zip(offsets, pairs, strict=True))
    offsets = [0] + sorted(offsets[1:], reverse=True)
    back = [swap_ranks(pairs[o], o) if o else pairs[o] for o in offsets]
    columns, chosen = on_core(
        functools.partial(select_kernel, plan, offsets, shards),
        place,
        (weights,),
        [((len(offsets) * weights.shape[0], 128), F32), ((8 * PARTS, weights.shape[0]), BF16)],
        half,
    )
    own, other = on_core(
        finish_kernel,
        None,
        (columns, chosen, *back),
        [((4 * PARTS, half // PARTS), BF16)] * 2,
        half,
    )
    own, other = unfolded(own), unfolded(swap_cores(other))
    whole = jnp.where(
        core == 0,
        jnp.concatenate([own, other], axis=1),
        jnp.concatenate([other, own], axis=1),
    )
    return (whole[None, :2], whole[None, 2:])


def solution(mesh):
    return jax.shard_map(
        local,
        mesh=mesh,
        in_specs=(
            P("section", "expert", None),
            P("section", "expert", None),
            P("section", "expert", None),
            P("section", "expert", None),
            P("section", "expert", None),
            P("section", "expert", None),
            P("section", "expert", None),
            P(None, "expert"),
            P(None, "expert"),
            P("expert", None),
        ),
        out_specs=(P("section", "expert", None), P("section", "expert", None)),
        check_vma=False,
    )
```

```python
import functools
import typing

import jax
import jax.numpy as jnp
from jax import lax
from jax.experimental import pallas as pl
from jax.experimental.pallas import tpu as pltpu
from jax.sharding import PartitionSpec as P

GROUPS = 4
PARTS = 4
BATCH = 8
F32 = jnp.float32
BF16 = jnp.bfloat16


def swap_cores(block):
    sections = range(lax.axis_size("section"))
    return lax.ppermute(block, "section", [(i, i ^ 1) for i in sections])


def expert_weights(routes, probs):
    named = routes[:, :, None] == jnp.arange(GROUPS, dtype=jnp.int32)
    return jnp.sum(jnp.where(named, probs[:, :, None], 0.0), axis=1)


def by_section(mine, theirs, core):
    return jnp.where(core == 0, mine, theirs), jnp.where(core == 0, theirs, mine)


def swap_ranks(block, bit):
    ranks = range(lax.axis_size("expert"))
    return lax.ppermute(block, "expert", [(i, i ^ bit) for i in ranks])


def to_next_chips(fwd, bwd, bit):
    sections, ranks = lax.axis_size("section"), lax.axis_size("expert")

    def move(block, pairs):
        route = [(a * ranks + e, b * ranks + (e ^ bit)) for a, b in pairs for e in range(ranks)]
        return lax.ppermute(block, ("section", "expert"), route)

    up = [(i, i + 2) for i in range(sections - 2)]
    down = [(b, a) for a, b in up]
    if sections != 4:
        return [move(fwd, up), move(bwd, down)]
    return [move(jnp.where(lax.axis_index("section") < 2, fwd, bwd), up + down)]


def folded(block):
    rows, width = block.shape
    block = block.reshape(rows, PARTS, width // PARTS).transpose(1, 0, 2)
    return block.reshape(rows * PARTS, width // PARTS)


def unfolded(block):
    rows, width = block.shape
    block = block.reshape(PARTS, rows // PARTS, width).transpose(1, 0, 2)
    return block.reshape(rows // PARTS, width * PARTS)


class Plan(typing.NamedTuple):
    fwd: int
    both: int
    bwd: int
    rows: int
    places: tuple
    other: tuple


def plan_of(sections):
    if sections == 4:
        places = ((0, 2, 0), (24, 4, 0), (8, 4, 0), (24, 4, 2), (8, 4, 2))
        other = (None, (24, 2, 0), None, (32, 2, 0), None)
        return Plan(1, 1, 1, 40, places, other)
    places = ((0, 2, 0), (24, 2, 0), (8, 4, 0), (32, 4, 0), (8, 4, 2), (32, 4, 2))
    return Plan(2, 0, 2, 48, places, (None,) * 6)


def dot(a, b):
    return jnp.dot(a, b, preferred_element_type=F32)


def one_hot(rows, want):
    out = lax.broadcasted_iota(jnp.int32, (rows, rows), 0)
    src = lax.broadcasted_iota(jnp.int32, (rows, rows), 1)
    return jnp.where(want(out) == src, 1.0, 0.0).astype(BF16)


def gathered_order(plan, forward):
    kinds = len(plan.places)

    def want(out):
        part, rest = lax.div(out, kinds * 2 * BATCH), lax.rem(out, kinds * 2 * BATCH)
        kind, rest = lax.div(rest, 2 * BATCH), lax.rem(rest, 2 * BATCH)
        row = jnp.zeros_like(out)
        for i, (here, there) in enumerate(zip(plan.places, plan.other, strict=True)):
            base, size, offset = here
            if there is not None:
                base, size, offset = (
                    jnp.where(forward == 1, t, h) for h, t in zip(here, there, strict=True)
                )
            row = jnp.where(kind == i, base + offset + part * size, row)
        return lax.div(rest, 2) * plan.rows + row + lax.rem(rest, 2)

    return one_hot(BATCH * plan.rows, want)


def returned_order(groups):
    size = PARTS * groups * 2

    def want(out):
        block, rest = lax.div(out, size), lax.rem(out, size)
        return lax.div(rest, 2) * (2 * BATCH) + block * 2 + lax.rem(rest, 2)

    return one_hot(BATCH * size, want)


class Piece(typing.NamedTuple):
    weight: int
    axis: int
    start: int
    size: int
    steps: int


def fetch_kernel(pieces, order, place, *refs):
    count = 1 + max(piece.weight for piece in pieces)
    weights, refs = refs[:count], refs[count + 1 :]
    *outs, zero, made, sems = refs
    copies = []
    for i, piece in enumerate(pieces):
        weight, held = weights[piece.weight], outs[2 * i]
        half = weight.shape[piece.axis] // 2
        size = piece.size // piece.steps
        for step in range(piece.steps):
            start = place[0] * half + piece.start + step * size
            there = pl.ds(pl.multiple_of(start, 128), size)
            here = pl.ds(step * size, size)
            if piece.axis == 1:
                there, here = (slice(None), there), (slice(None), here)
            sem = sems.at[len(copies)]
            copies.append(pltpu.make_async_copy(weight.at[there], held.at[here], sem))
    for copy in copies:
        copy.start()
    zero[...] = jnp.zeros_like(zero)
    made[...] = order(place)
    copies = iter(copies)
    for i, piece in enumerate(pieces):
        held, turned = outs[2 * i : 2 * i + 2]
        size = piece.size // piece.steps
        for step in range(piece.steps):
            next(copies).wait()
            here = slice(step * size, (step + 1) * size)
            if piece.axis == 0:
                turned[:, here] = held[here, :].T
            else:
                turned[here, :] = held[:, here].T


def fetch(place, weights, pieces, earlier, like, order, count):
    shapes = []
    for piece in pieces:
        shape = list(weights[piece.weight].shape)
        shape[piece.axis] = piece.size
        shapes += [tuple(shape), tuple(shape[::-1])]
    nbytes = sum(piece.size for piece in pieces) * weights[0].shape[1] * 4
    steps = sum(piece.steps for piece in pieces)
    return pl.pallas_call(
        functools.partial(fetch_kernel, pieces, order),
        in_specs=[pl.BlockSpec(memory_space=pltpu.SMEM)]
        + [pl.BlockSpec(memory_space=pltpu.HBM)] * len(weights)
        + [pl.BlockSpec(memory_space=pl.ANY)],
        out_specs=[pl.BlockSpec(memory_space=pltpu.VMEM)] * (len(shapes) + 2),
        out_shape=[pltpu.VMEM(shape, BF16) for shape in shapes]
        + [jax.ShapeDtypeStruct(like, BF16), pltpu.VMEM((count, count), BF16)],
        scratch_shapes=[pltpu.SemaphoreType.DMA((steps,))],
        compiler_params=pltpu.CompilerParams(vmem_limit_bytes=2**21),
        cost_estimate=pl.CostEstimate(flops=0, bytes_accessed=nbytes, transcendentals=0),
    )(
        place,
        *[pltpu.with_memory_space_constraint(weight, pltpu.HBM) for weight in weights],
        earlier,
    )


def up_kernel(plan, ranks, order, first, second, third, fourth, g, u_low, u_high, d_t, out):
    hid = g.shape[1]
    n = 2 * BATCH
    kinds = len(plan.places)
    groups = plan.fwd + plan.both + plan.bwd
    piece = first.shape[1]
    blocks = jnp.concatenate([first[...], second[...], third[...], fourth[...]])
    order = order[...]
    count = order.shape[0]
    batches = ranks // BATCH
    sorted_rows = [
        dot(order, blocks[i * count : (i + 1) * count]).astype(BF16) for i in range(batches)
    ]
    a, b, dh = 0.0, 0.0, 0.0
    for part in range(PARTS):
        cols = slice(part * piece, (part + 1) * piece)
        at = [(part * kinds + kind) * n for kind in range(kinds)]
        taken = [jnp.concatenate([rows[i : i + n] for rows in sorted_rows]) for i in at]
        rows = jnp.concatenate(taken[:groups])
        a += dot(rows, g[cols, :])
        u = u_high[(part - 1) * piece : part * piece, :] if part else u_low[...]
        b += dot(rows, u)
        dh += dot(jnp.concatenate(taken[groups:]), d_t[cols, :])
    n = n * batches
    for i in range(groups):
        out[:, i * hid : (i + 1) * hid] = a[i * n : (i + 1) * n]
        out[:, (groups + i) * hid : (groups + i + 1) * hid] = b[i * n : (i + 1) * n]
    for i in range(kinds - groups):
        at = (2 * groups + i) * hid
        out[:, at : at + hid] = dh[i * n : (i + 1) * n]


def down_kernel(plan, ranks, place, _, order, mine, theirs, g_t, u_t_low, u_t_high, d, kept, sent):
    hid = d.shape[0]
    groups = plan.fwd + plan.both + plan.bwd
    n = 2 * ranks
    split = plan.fwd * n

    def summed(i):
        return mine[:, i * hid : (i + 1) * hid] + theirs[:, i * hid : (i + 1) * hid]

    h, da, du = [], [], []
    forward = jnp.where(place[2] == 1, 1.0, 0.0)
    for i in range(groups):
        a, b = summed(i), summed(groups + i)
        s = jax.nn.sigmoid(a)
        if i < plan.fwd + plan.both:
            hidden = (a * s * b).astype(BF16)
            h.append(hidden if i < plan.fwd else hidden * forward.astype(BF16))
        if i >= plan.fwd:
            dh = summed(2 * groups + i - plan.fwd)
            da.append((dh * b * s * (1.0 + a * (1.0 - s))).astype(BF16))
            du.append((dh * a * s).astype(BF16))
    h, da, du = jnp.concatenate(h), jnp.concatenate(da), jnp.concatenate(du)
    piece = kept.shape[1]
    results = []
    for part in range(PARTS):
        cols = slice(part * piece, (part + 1) * piece)
        y = dot(h, d[:, cols])
        u_t = u_t_high[:, (part - 1) * piece : part * piece] if part else u_t_low[...]
        dx = dot(da, g_t[:, cols]) + dot(du, u_t)
        shared = plan.both * n
        rows = [y[:split], y[split:] + dx[:shared], dx[shared:]] if shared else [y, dx]
        results.append(jnp.concatenate(rows).astype(BF16))
    order = order[...]
    size = 2 * BATCH
    rows = [
        jnp.concatenate(
            [
                result[i * n + batch * size : i * n + (batch + 1) * size]
                for result in results
                for i in range(groups)
            ]
        )
        for batch in range(ranks // BATCH)
    ]
    rows = jnp.concatenate([dot(order, batch).astype(BF16) for batch in rows])
    kept[...] = rows[: kept.shape[0]]
    sent[...] = rows[kept.shape[0] :]


def pair_kernel(kept, got, weights, *pairs):
    size = pairs[0].shape[0]
    total = kept[...].astype(F32) + got[...].astype(F32)
    for i, pair in enumerate(pairs):
        pair[...] = total[i * size : (i + 1) * size].astype(BF16)


def select_kernel(plan, offsets, shards, place, weights, columns, chosen):
    size = weights.shape[0]
    for i, offset in enumerate(offsets):
        expert = lax.div(lax.bitwise_xor(place[1], jnp.int32(offset)), jnp.int32(shards))
        named = lax.broadcasted_iota(jnp.int32, weights.shape, 1) == expert
        weight = jnp.sum(jnp.where(named, weights[...], 0.0), axis=1, keepdims=True)
        columns[i * size : (i + 1) * size, :] = jnp.broadcast_to(weight, (size, 128))
    out = lax.broadcasted_iota(jnp.int32, chosen.shape, 0)
    src = lax.broadcasted_iota(jnp.int32, chosen.shape, 1)
    odd = jnp.where(out < 4 * PARTS, place[0], 1 - place[0])
    part, row = lax.rem(lax.div(out, 4), PARTS), lax.rem(out, 4)
    bwd = lax.div(row, 2)
    if plan.both:
        far = jnp.where(place[2] == 1, 0, 1)
        group = jnp.where(bwd == odd, 1, 2 * bwd)
        present = (bwd != odd) | (bwd == far)
    else:
        group = 2 * bwd + jnp.where(bwd == odd, 1, 0)
        present = out >= 0
    groups = plan.fwd + plan.both + plan.bwd
    want = part * (2 * groups) + group * 2 + lax.rem(row, 2)
    chosen[...] = jnp.where((want == src) & present, 1.0, 0.0).astype(BF16)


def finish_kernel(columns, chosen, *refs):
    *back, own, other = refs
    size = back[0].shape[0]
    total = 0.0
    for i, block in enumerate(back):
        total += block[...].astype(F32) * columns[i * size : (i + 1) * size, :1]
    rows = dot(chosen[...], total.astype(BF16)).astype(BF16)
    own[...] = rows[: own.shape[0]]
    other[...] = rows[own.shape[0] :]


def on_core(kernel, place, operands, results, cost):
    specs = [pl.BlockSpec(memory_space=pltpu.VMEM)] * len(operands)
    operands = [pltpu.with_memory_space_constraint(x, pltpu.VMEM) for x in operands]
    if place is not None:
        specs = [pl.BlockSpec(memory_space=pltpu.SMEM)] + specs
        operands = [place] + operands
    ranks = lax.axis_size("expert")
    return pl.pallas_call(
        kernel,
        in_specs=specs,
        out_specs=[pl.BlockSpec(memory_space=pltpu.VMEM)] * len(results),
        out_shape=[jax.ShapeDtypeStruct(*result) for result in results],
        compiler_params=pltpu.CompilerParams(vmem_limit_bytes=ranks * 3 * 2**17),
        cost_estimate=pl.CostEstimate(
            flops=cost * 512, bytes_accessed=cost * 2, transcendentals=0
        ),
    )(*operands)


def after(value, other):
    return lax.optimization_barrier((value, other))[0]


def local(
    fwd_tokens,
    fwd_routes,
    fwd_probs,
    bwd_tokens,
    bwd_routes,
    bwd_probs,
    bwd_grads,
    w_gate,
    w_up,
    w_down,
):
    ranks, sections = lax.axis_size("expert"), lax.axis_size("section")
    shards = ranks // GROUPS
    plan = plan_of(sections)
    groups = plan.fwd + plan.both + plan.bwd
    width = fwd_tokens.shape[2]
    half = width // 2
    hid = w_gate.shape[1]
    section = lax.axis_index("section")
    core = section % 2
    place = jnp.stack([core, lax.axis_index("expert"), section >= 2]).astype(jnp.int32)

    inputs = [fwd_tokens[0], bwd_tokens[0], bwd_grads[0]]
    theirs = jnp.concatenate([swap_cores(block) for block in inputs])
    mine = jnp.concatenate(inputs)
    mine, theirs = (
        jnp.where(core == 0, rows[:, :half], rows[:, half:]) for rows in (mine, theirs)
    )
    even, odd = by_section(mine, theirs, core)

    near = jnp.concatenate([folded(even[:2]), folded(odd[2:])])
    far_fwd, far_bwd = folded(odd[:2]), folded(even[2:])
    if plan.both:
        far_fwd = jnp.pad(far_fwd, ((0, far_bwd.shape[0] - far_fwd.shape[0]), (0, 0)))
    top = ranks // 2
    far = to_next_chips(far_fwd, far_bwd, 0)
    far_top = to_next_chips(far_fwd, far_bwd, top)
    blocks = jnp.concatenate([near, *far, swap_ranks(near, top), *far_top])
    offsets = [0, top]
    piece = half // PARTS
    g, g_t, u_low, u_t_low, zero, back_order = fetch(
        place,
        (w_gate, w_up),
        (Piece(0, 0, 0, half, 4), Piece(1, 0, 0, piece, 1)),
        near,
        blocks.shape,
        lambda _: returned_order(groups),
        BATCH * PARTS * groups * 2,
    )
    blocks = blocks + zero
    bit = top // 2
    while bit > 2:
        blocks = jnp.concatenate([blocks, swap_ranks(blocks, bit)])
        offsets += [o ^ bit for o in offsets]
        bit //= 2
    offsets += [o ^ 2 for o in offsets]
    fourth = swap_ranks(blocks, 3)
    second = swap_ranks(blocks, 2)
    third = swap_ranks(blocks, 1)
    d, d_t, u_high, u_t_high, _, got_order = fetch(
        place,
        (w_up, w_down),
        (Piece(1, 1, 0, half, 4), Piece(0, 0, piece, half - piece, 3)),
        blocks,
        (16, 128),
        lambda place: gathered_order(plan, place[2]),
        BATCH * plan.rows,
    )

    (mine,) = on_core(
        functools.partial(up_kernel, plan, ranks),
        None,
        (got_order, blocks, second, third, fourth, g, u_low, u_high, d_t),
        [((2 * ranks, (groups + len(plan.places)) * hid), F32)],
        3 * hid * half,
    )
    weights = jnp.concatenate(
        [
            expert_weights(after(fwd_routes[0], mine), fwd_probs[0]),
            expert_weights(after(bwd_routes[0], mine), bwd_probs[0]),
        ]
    )
    others = swap_cores(weights)
    even, odd = by_section(weights, others, core)
    kept, sent = on_core(
        functools.partial(down_kernel, plan, ranks),
        place,
        (others, back_order, mine, swap_cores(mine), g_t, u_t_low, u_t_high, d),
        [((ranks // 2 * PARTS * groups * 2, half // PARTS), BF16)] * 2,
        3 * hid * half,
    )
    far = to_next_chips(odd[:2], even[2:], 0)
    weights = jnp.concatenate([even[:2], far[0], odd[2:], *far[1:]])
    weights = jnp.concatenate([weights] * PARTS)
    block = ((PARTS * groups * 2, half // PARTS), BF16)
    pairs = on_core(
        pair_kernel, None, (kept, swap_ranks(sent, 1), weights), [block] * (ranks // 2), half
    )
    pairs = dict(zip(offsets, pairs, strict=True))
    offsets = [0] + sorted(offsets[1:], reverse=True)
    back = [swap_ranks(pairs[o], o) if o else pairs[o] for o in offsets]
    columns, chosen = on_core(
        functools.partial(select_kernel, plan, offsets, shards),
        place,
        (weights,),
        [((len(offsets) * weights.shape[0], 128), F32), ((8 * PARTS, weights.shape[0]), BF16)],
        half,
    )
    own, other = on_core(
        finish_kernel,
        None,
        (columns, chosen, *back),
        [((4 * PARTS, half // PARTS), BF16)] * 2,
        half,
    )
    own, other = unfolded(own), unfolded(swap_cores(other))
    whole = jnp.where(
        core == 0,
        jnp.concatenate([own, other], axis=1),
        jnp.concatenate([other, own], axis=1),
    )
    return (whole[None, :2], whole[None, 2:])


def solution(mesh):
    return jax.shard_map(
        local,
        mesh=mesh,
        in_specs=(
            P("section", "expert", None),
            P("section", "expert", None),
            P("section", "expert", None),
            P("section", "expert", None),
            P("section", "expert", None),
            P("section", "expert", None),
            P("section", "expert", None),
            P(None, "expert"),
            P(None, "expert"),
            P("expert", None),
        ),
        out_specs=(P("section", "expert", None), P("section", "expert", None)),
        check_vma=False,
    )
```
